128 devices in a mesh: layer: 4 (over x_hi, core), prow: 2 (over x_lo), pcol: 16 (over z, y).
Axes of the slice: x: 4 (x_hi: 2, x_lo: 2; x = x_hi * 2 + x_lo), y: 4, z: 4, core: 2. Of those that a mesh axis runs over, the one named last changes fastest.
Arguments:
- sub_rhs: float32 [4, 2, 16, 5, 32, 128], P('layer', 'prow', 'pcol'), may hold values from -6 to 6
- sub_lower_inverse: float32 [4, 2, 16, 5, 128, 128], P('layer', 'prow', 'pcol')
- sub_upper_inverse: float32 [4, 2, 16, 5, 128, 128], P('layer', 'prow', 'pcol')
- sub_lower: bfloat16 [4, 2, 16, 5, 16, 128, 128], P('layer', 'prow', 'pcol'), may hold values from -0.078125 to 0.078125
- sub_upper: bfloat16 [4, 2, 16, 5, 16, 128, 128], P('layer', 'prow', 'pcol'), may hold values from -0.078125 to 0.078125
- sub_source: int32 [4, 2, 16, 5, 16], P('layer', 'prow', 'pcol'), may hold values from 0 to 1
- sub_target: int32 [4, 2, 16, 5, 16], P('layer', 'prow', 'pcol'), may hold values from 0 to 31
- top_rhs: float32 [2, 16, 3, 32, 128], P('prow', 'pcol'), may hold values from -6 to 6
- top_lower_inverse: float32 [2, 16, 3, 128, 128], P('prow', 'pcol')
- top_upper_inverse: float32 [2, 16, 3, 128, 128], P('prow', 'pcol')
- top_lower: bfloat16 [2, 16, 2, 16, 128, 128], P('prow', 'pcol'), may hold values from -0.078125 to 0.078125
- top_upper: bfloat16 [2, 16, 2, 16, 128, 128], P('prow', 'pcol'), may hold values from -0.078125 to 0.078125
- top_source: int32 [2, 16, 2, 16], P('prow', 'pcol'), may hold values from 0 to 1
- top_target: int32 [2, 16, 2, 16], P('prow', 'pcol'), may hold values from 0 to 31, as said below
Outputs:
- sub_solution: float32 [4, 2, 16, 5, 32, 128], P('layer', 'prow', 'pcol')
- top_solution: float32 [2, 16, 3, 32, 128], P('prow', 'pcol')
The draws below stay inside these ranges and needn't reach their ends.
Inputs may be any that keep to these rules, and one draw needn't show every extreme that they name: `top_target`: at the last ancestor level of slots every code is below 16.
All inputs are finite; a program needn't handle non-finite values.
Results may differ from the reference program's by a relative error of at most 0.015.
Values may be sent and summed in bfloat16 or wider, within the bound.
A program may use at most 64 MiB of HBM per device.

```python
import jax
import jax.numpy as jnp
from jax import lax

WIDTH = 128
SIDES = 32
SLOTS = 16
SUB = 5
TOP = 3
LAYERS = 4
ROWS = 2
COLS = 16


def inverse_blocks(key, leading):
    identity = jnp.eye(WIDTH, dtype=jnp.float32)
    jitter = jax.random.normal(key, leading + (WIDTH, WIDTH), jnp.float32) * (0.45 / WIDTH ** 0.5)
    return identity + jitter


def draw_sub_lower_inverse(key, part):
    return inverse_blocks(jax.random.fold_in(key, 11), (LAYERS, ROWS, COLS, SUB))


def draw_sub_upper_inverse(key, part):
    return inverse_blocks(jax.random.fold_in(key, 23), (LAYERS, ROWS, COLS, SUB))


def draw_top_lower_inverse(key, part):
    return inverse_blocks(jax.random.fold_in(key, 37), (ROWS, COLS, TOP))


def draw_top_upper_inverse(key, part):
    return inverse_blocks(jax.random.fold_in(key, 53), (ROWS, COLS, TOP))


def draw_top_target(key, part):
    target_codes = jax.random.randint(jax.random.fold_in(key, 71), (ROWS, COLS, TOP - 1, SLOTS), 0, 2 * COLS)
    final_codes = target_codes[:, :, TOP - 2] % COLS
    return target_codes.at[:, :, TOP - 2].set(final_codes)


def set_ends(entries, rng, low, largest):
    longest = entries.shape.index(max(entries.shape))
    spots = []
    for shift in (0, 1):
        where = [jax.random.randint(jax.random.fold_in(rng, axis), (), 0, length) for axis, length in enumerate(entries.shape)]
        where[longest] = (where[longest] + shift) % entries.shape[longest]
        spots.append(tuple(where))
    return entries.at[spots[0]].set(low).at[spots[1]].set(largest)


def level_of(stream_key, extent, pieces, least, high):
    def one(position, shards_of):
        steps = jax.random.uniform(jax.random.fold_in(jax.random.fold_in(stream_key, 6), position), (shards_of,), jnp.float32, least / len(pieces), high / len(pieces))
        return jnp.repeat(jnp.exp(steps), extent[position] // shards_of).reshape((-1,) + (1,) * (len(extent) - position - 1))

    gain = one(*pieces[0])
    for cut in pieces[1:]:
        gain = gain * one(*cut)
    return gain


def scatter_about(key, shape, scale, limit, cuts=(), kind=jnp.bfloat16):
    entries = jax.random.normal(key, shape, jnp.float32) * scale
    if len(cuts) > 0:
        entries = level_of(key, shape, cuts, -0.22, 0.18) * entries
    return jnp.clip(entries, min=-limit, max=limit).astype(kind)


def setup_inputs(seed: int = 0) -> dict:
    arg_keys = jax.random.split(jax.random.key(seed), 15)
    sub_rhs = scatter_about(arg_keys[0], (LAYERS, ROWS, COLS, SUB, SIDES, WIDTH), 1.0, 6.0, ((0, 4), (1, 2), (2, 16)), jnp.float32)
    sub_lower_inverse = draw_sub_lower_inverse(jax.random.fold_in(arg_keys[14], 71), 0)
    sub_upper_inverse = draw_sub_upper_inverse(jax.random.fold_in(arg_keys[14], 71), 0)
    sub_lower = scatter_about(arg_keys[3], (LAYERS, ROWS, COLS, SUB, SLOTS, WIDTH, WIDTH), (3 * WIDTH * SLOTS) ** -0.5, 0.078125, ((0, 4), (1, 2), (2, 16)))
    sub_upper = scatter_about(arg_keys[4], (LAYERS, ROWS, COLS, SUB, SLOTS, WIDTH, WIDTH), (3 * WIDTH * SLOTS) ** -0.5, 0.078125, ((0, 4), (1, 2), (2, 16)))
    sub_source = set_ends(jax.random.randint(arg_keys[5], (LAYERS, ROWS, COLS, SUB, SLOTS), 0, ROWS), jax.random.fold_in(arg_keys[5], 1), 0, ROWS - 1).astype(jnp.int32)
    sub_target = set_ends(jax.random.randint(arg_keys[6], (LAYERS, ROWS, COLS, SUB, SLOTS), 0, 2 * COLS), jax.random.fold_in(arg_keys[6], 1), 0, (2 * COLS) - 1).astype(jnp.int32)
    top_rhs = scatter_about(arg_keys[7], (ROWS, COLS, TOP, SIDES, WIDTH), 1.0, 6.0, ((0, 2), (1, 16)), jnp.float32)
    top_lower_inverse = draw_top_lower_inverse(jax.random.fold_in(arg_keys[14], 71), 0)
    top_upper_inverse = draw_top_upper_inverse(jax.random.fold_in(arg_keys[14], 71), 0)
    top_lower = scatter_about(arg_keys[10], (ROWS, COLS, TOP - 1, SLOTS, WIDTH, WIDTH), (3 * WIDTH * SLOTS) ** -0.5, 0.078125, ((0, 2), (1, 16)))
    top_upper = scatter_about(arg_keys[11], (ROWS, COLS, TOP - 1, SLOTS, WIDTH, WIDTH), (3 * WIDTH * SLOTS) ** -0.5, 0.078125, ((0, 2), (1, 16)))
    top_source = set_ends(jax.random.randint(arg_keys[12], (ROWS, COLS, TOP - 1, SLOTS), 0, ROWS), jax.random.fold_in(arg_keys[12], 1), 0, ROWS - 1).astype(jnp.int32)
    top_target = draw_top_target(jax.random.fold_in(arg_keys[14], 71), 0)
    return {"sub_rhs": sub_rhs, "sub_lower_inverse": sub_lower_inverse, "sub_upper_inverse": sub_upper_inverse, "sub_lower": sub_lower, "sub_upper": sub_upper, "sub_source": sub_source, "sub_target": sub_target, "top_rhs": top_rhs, "top_lower_inverse": top_lower_inverse, "top_upper_inverse": top_upper_inverse, "top_lower": top_lower, "top_upper": top_upper, "top_source": top_source, "top_target": top_target}


def apply_inverse(remainder, inverse):
    return jnp.einsum('...qw,...wv->...qv', remainder, inverse, precision=lax.Precision.HIGHEST)


def rounded_copy(values):
    return lax.optimization_barrier(values.astype(jnp.bfloat16)).astype(jnp.float32)


def forward_terms(values, blocks, source, target):
    rounded = rounded_copy(values)
    chooser = jax.nn.one_hot(source, ROWS, dtype=jnp.float32)
    picked = jnp.einsum('...rckj,...jcqw->...rckqw', chooser, rounded, precision=lax.Precision.HIGHEST)
    products = jnp.einsum('...rckqw,...rckwv->...rckqv', picked, blocks.astype(jnp.float32), precision=lax.Precision.HIGHEST)
    target_hot = jax.nn.one_hot(target, 2 * COLS, dtype=jnp.float32)
    shares = jnp.einsum('...rckt,...rckqv->...rtqv', target_hot, products, precision=lax.Precision.HIGHEST)
    return shares.reshape(shares.shape[:-3] + (2, COLS) + shares.shape[-2:])


def backward_terms(ahead_values, blocks, source, target):
    target_hot = jax.nn.one_hot(target, 2 * COLS, dtype=jnp.float32)
    picked = jnp.einsum('...rckt,...rtqw->...rckqw', target_hot, ahead_values, precision=lax.Precision.HIGHEST)
    products = jnp.einsum('...rckqw,...rckwv->...rckqv', picked, blocks.astype(jnp.float32), precision=lax.Precision.HIGHEST)
    chooser = jax.nn.one_hot(source, ROWS, dtype=jnp.float32)
    return jnp.einsum('...rckj,...rckqv->...jcqv', chooser, products, precision=lax.Precision.HIGHEST)


def reference(sub_rhs, sub_lower_inverse, sub_upper_inverse, sub_lower, sub_upper, sub_source, sub_target,
              top_rhs, top_lower_inverse, top_upper_inverse, top_lower, top_upper, top_source, top_target):
    nothing_sub = jnp.zeros((LAYERS, ROWS, COLS, SIDES, WIDTH), jnp.float32)
    nothing_top = jnp.zeros((ROWS, COLS, SIDES, WIDTH), jnp.float32)
    pending_sub = [nothing_sub] * SUB
    pending_top = [nothing_top] * TOP
    solved_sub = []
    solved_top = []
    for height in range(SUB):
        values = apply_inverse(sub_rhs[:, :, :, height] - pending_sub[height], sub_lower_inverse[:, :, :, height])
        solved_sub.append(values)
        shares = forward_terms(values, sub_lower[:, :, :, height], sub_source[:, :, :, height], sub_target[:, :, :, height])
        for offset in range(2):
            destination = height + 1 + offset
            if destination < SUB:
                pending_sub[destination] = pending_sub[destination] + shares[:, :, offset]
            else:
                pending_top[destination - SUB] = pending_top[destination - SUB] + jnp.sum(shares[:, :, offset], axis=0)
    for height in range(TOP):
        values = apply_inverse(top_rhs[:, :, height] - pending_top[height], top_lower_inverse[:, :, height])
        solved_top.append(values)
        if height < TOP - 1:
            shares = forward_terms(values, top_lower[:, :, height], top_source[:, :, height], top_target[:, :, height])
            for offset in range(2):
                destination = height + 1 + offset
                if destination < TOP:
                    pending_top[destination] = pending_top[destination] + shares[:, offset]
    finish_top = [None] * TOP
    rounded_top = [None] * TOP
    for height in reversed(range(TOP)):
        remainder = solved_top[height]
        if height < TOP - 1:
            nearer = rounded_top[height + 1]
            farther = rounded_top[height + 2] if height + 2 < TOP else nothing_top
            ahead_values = jnp.stack([nearer, farther], axis=1).reshape(ROWS, 2 * COLS, SIDES, WIDTH)
            remainder = remainder - backward_terms(ahead_values, top_upper[:, :, height], top_source[:, :, height], top_target[:, :, height])
        values = apply_inverse(remainder, top_upper_inverse[:, :, height])
        finish_top[height] = values
        rounded_top[height] = rounded_copy(values)
    finish_sub = [None] * SUB
    rounded_sub = [None] * SUB

    def rounded_at(height):
        if height < SUB:
            return rounded_sub[height]
        return jnp.broadcast_to(rounded_top[height - SUB], (LAYERS, ROWS, COLS, SIDES, WIDTH))

    for height in reversed(range(SUB)):
        ahead_values = jnp.stack([rounded_at(height + 1), rounded_at(height + 2)], axis=2)
        ahead_values = ahead_values.reshape(LAYERS, ROWS, 2 * COLS, SIDES, WIDTH)
        remainder = solved_sub[height] - backward_terms(ahead_values, sub_upper[:, :, :, height], sub_source[:, :, :, height], sub_target[:, :, :, height])
        values = apply_inverse(remainder, sub_upper_inverse[:, :, :, height])
        finish_sub[height] = values
        rounded_sub[height] = rounded_copy(values)
    return jnp.stack(finish_sub, axis=3), jnp.stack(finish_top, axis=2)
```

```python
import jax
import jax.numpy as jnp
from jax import lax
from jax.experimental import pallas as pl
from jax.experimental.pallas import tpu as pltpu
from jax.sharding import PartitionSpec as P

MESH = pl.DeviceIdType.MESH
F32 = jnp.float32
BF16 = jnp.bfloat16
SUB, TOP, SLOTS, COLS, SIDES, WIDTH = 5, 3, 16, 16, 32, 128
HALF = SIDES // 2
LINKED = SUB + TOP - 1
ORDER = (10, 9, 11, 6, 14, 5, 7, 13, 15, 8, 2, 1, 3, 4, 12, 0)


def dot(a, b):
    return jnp.dot(a, b, preferred_element_type=F32)


def dot_full(a, b):
    return jnp.dot(a, b, preferred_element_type=F32, precision=lax.Precision.HIGHEST)


def dot_split(a, b):
    high = a.astype(BF16)
    low = (a - high.astype(F32)).astype(BF16)
    return dot(high, b) + dot(low, b)


def wait_for(ref, sem):
    pltpu.make_async_copy(ref, ref, sem).wait()


def kernel(
    sub_rhs, sub_linv, sub_uinv, sub_lower, sub_upper, sub_src, sub_tgt,
    top_rhs, top_linv, top_uinv, top_lower, top_upper, top_src, top_tgt,
    sub_out, top_out,
    lower, upper, linv, uinv, rhs_sub, rhs_top,
    linv_low, uinv_low, linv_other, uinv_other, rhs_sub_other, rhs_top_other,
    perm, psrc, ends,
    ylow, ylow_other, y_sub, y_top, sums, pend, pend_top,
    send_f, recv_f, send_ft, recv_5, recv_ft,
    halves, core_out, core_in, six,
    x_sub, x_top, send_b, recv_b, send_bt, recv_7, recv_6, recv_b5, six_in, six_out, last_out, last_in, top_mine, top_other,
    load_sem, lin_sem, misc_recv, misc_send, rf_sem, sf_sem, rb_sem, sb_sem,
):
    l, r, c = lax.axis_index("layer"), lax.axis_index("prow"), lax.axis_index("pcol")
    high, half = l // 2, l % 2
    half_rows = pl.ds(pl.multiple_of(half * HALF, HALF), HALF)
    me = r * COLS + c

    loads = (
        (sub_lower, lower.at[pl.ds(0, SUB)]),
        (top_lower, lower.at[pl.ds(SUB, TOP - 1)]),
        (sub_upper, upper.at[pl.ds(0, SUB)]),
        (top_upper, upper.at[pl.ds(SUB, TOP - 1)]),
        (sub_linv, linv.at[pl.ds(0, SUB)]),
        (top_linv, linv.at[pl.ds(SUB, TOP)]),
        (sub_uinv, uinv.at[pl.ds(0, SUB)]),
        (top_uinv, uinv.at[pl.ds(SUB, TOP)]),
        (sub_rhs, rhs_sub),
        (top_rhs.at[:, half_rows], rhs_top),
    )
    copies = [pltpu.make_async_copy(a, b, load_sem.at[i]) for i, (a, b) in enumerate(loads)]
    for i in (8, 4, 5, 6, 7, 9, 0, 1, 2, 3):
        copies[i].start()

    barrier = pltpu.get_barrier_semaphore()
    for flip in (0, 1, 2):
        for j in range(2):
            for i in range(COLS):
                if flip or j or i:
                    pl.semaphore_signal(barrier, inc=1, device_id=(l ^ flip, r ^ j, c ^ i), device_id_type=MESH)

    def sort_level(src, tgt, row, t):
        codes = [tgt[row, k] for k in range(SLOTS)]
        rank = [jnp.int32(0)] * SLOTS
        for k in range(SLOTS):
            for j in range(k):
                before = (codes[j] <= codes[k]).astype(jnp.int32)
                rank[k] = rank[k] + before
                rank[j] = rank[j] + (1 - before)
        for i in range(SLOTS):
            slot = jnp.int32(0)
            for k in range(1, SLOTS):
                slot = slot + jnp.where(rank[k] == i, k, 0)
            perm[t, i] = slot
            psrc[t, i] = src[row, slot]
        ends[t, 0] = 0
        for q in range(2 * COLS):
            count = jnp.int32(0)
            for k in range(SLOTS):
                count = count + (codes[k] <= q).astype(jnp.int32)
            ends[t, q + 1] = count

    @pl.loop(0, SUB)
    def _(t):
        sort_level(sub_src, sub_tgt, t, t)

    @pl.loop(0, TOP - 1)
    def _(t):
        sort_level(top_src, top_tgt, t, t + SUB)

    copies[8].wait()
    copies[4].wait()
    y0 = dot_full(rhs_sub[0], linv[0])
    y_sub[0] = y0
    ylow[r] = y0.astype(BF16)
    for i in (5, 6, 7, 9, 0, 1, 2, 3):
        copies[i].wait()

    @pl.loop(0, 6)
    def _(t):
        linv_low[t] = linv[t + 1].astype(BF16)
        uinv_low[t] = uinv[t + 1].astype(BF16)

    @pl.loop(0, COLS)
    def _(q):
        pend[q] = jnp.zeros((SIDES, WIDTH), F32)

    pl.semaphore_wait(barrier, 95)

    def to(device, src, dst, send_sem, recv_sem):
        copy = pltpu.make_async_remote_copy(
            src_ref=src, dst_ref=dst, send_sem=send_sem, recv_sem=recv_sem, device_id=device, device_id_type=MESH
        )
        copy.start()
        return copy

    other_row = (l, 1 - r, c)
    other_core = (l ^ 1, r, c)
    other_high = (l ^ 2, r, c)

    first = to(other_row, ylow.at[r], ylow_other, misc_send.at[0], misc_recv.at[0])
    lin_copies = [
        to(other_row, linv_low.at[t], linv_other.at[t], lin_sem.at[0, t], lin_sem.at[1, t]) for t in range(6)
    ]
    rhs_copy = to(
        other_row, rhs_sub.at[pl.ds(1, SUB - 1)], rhs_sub_other, misc_send.at[1], misc_recv.at[1]
    )
    rhs_top_copy = to(other_row, rhs_top.at[pl.ds(0, 2)], rhs_top_other, misc_send.at[2], misc_recv.at[2])

    def wait_linv(t):
        wait_for(linv_other.at[t - 1], lin_sem.at[1, t - 1])

    def products(t, rows):
        total = jnp.zeros((rows, WIDTH), F32)
        sums[0, :rows] = total
        for i in range(SLOTS):
            value = ylow[psrc[t, i]]
            total = total + dot(value[:rows], lower[t, perm[t, i]])
            sums[i + 1, :rows] = total

    def share(t, code, rows):
        return sums[ends[t, code + 1], :rows] - sums[ends[t, code], :rows]

    def forward(t):
        products(t, SIDES)
        for i in ORDER:
            q = c ^ i
            send_f[t, q] = (share(t, q, SIDES) + pend[q]).astype(BF16)
            for j in (1, 0):
                if i or j:
                    to((l, r ^ j, q), send_f.at[t, q], recv_f.at[t, me], sf_sem.at[t], rf_sem.at[t + 1])
        recv_f[t, me] = send_f[t, c]
        for q in range(COLS):
            pend[q] = share(t, COLS + q, SIDES)

    def add_up(ref, rows):
        parts = [ref[i].astype(F32) for i in range(COLS)]
        while len(parts) > 1:
            parts = [a + b for a, b in zip(parts[::2], parts[1::2])]
        return parts[0]

    def arrive(t):
        wait_for(recv_f.at[t - 1, pl.ds(0, 2 * COLS - 1)], rf_sem.at[t])
        wait_linv(t)
        mine = rhs_sub[t] - add_up(recv_f.at[t - 1, pl.ds(r * COLS, COLS)], SIDES)
        others = rhs_sub_other[t - 1] - add_up(recv_f.at[t - 1, pl.ds((1 - r) * COLS, COLS)], SIDES)
        y = dot_full(mine, linv[t])
        y_sub[t] = y
        ylow[r] = y.astype(BF16)
        ylow[1 - r] = dot_split(others, linv_other[t - 1]).astype(BF16)

    first.wait_recv()
    first.wait_send()
    ylow[1 - r] = ylow_other[...]
    forward(0)
    rhs_copy.wait_recv()

    @pl.loop(1, SUB - 1)
    def _(t):
        arrive(t)
        forward(t)

    t = SUB - 1
    arrive(t)
    products(t, SIDES)
    for q in range(COLS):
        both = share(t, q, SIDES) + pend[q]
        halves[0, 0, q] = both[:HALF]
        halves[0, 1, q] = both[HALF:]
    core_out[0] = halves[0, 1 - half].astype(BF16)
    core_copies = [to(other_core, core_out.at[0], core_in.at[0], misc_send.at[3], misc_recv.at[3])]
    for q in range(COLS):
        both = share(t, COLS + q, SIDES)
        halves[1, 0, q] = both[:HALF]
        halves[1, 1, q] = both[HALF:]
    core_out[1] = halves[1, 1 - half].astype(BF16)
    core_copies.append(to(other_core, core_out.at[1], core_in.at[1], misc_send.at[4], misc_recv.at[4]))
    core_copies[0].wait_recv()
    slot_5 = high * 2 * COLS + me
    for i in ORDER:
        q = c ^ i
        send_ft[0, q] = (halves[0, half, q] + core_in[0, q].astype(F32)).astype(BF16)
        for flip in (2, 0):
            for j in (1, 0):
                if i or j or flip:
                    to((l ^ flip, r ^ j, q), send_ft.at[0, q], recv_5.at[slot_5], sf_sem.at[t], rf_sem.at[t + 1])
    recv_5[slot_5] = send_ft[0, c]
    core_copies[1].wait_recv()
    six[high] = (halves[1, half] + core_in[1].astype(F32)).astype(BF16)
    six_copy = to(other_high, six.at[high], six.at[high], misc_send.at[5], misc_recv.at[5])
    upper_copy = to(other_row, uinv_low, uinv_other, misc_send.at[6], misc_recv.at[6])
    rhs_top_copy.wait_recv()
    six_copy.wait_recv()
    for q in range(COLS):
        pend_top[q] = six[0, q].astype(F32) + six[1, q].astype(F32)

    def arrive_top(t, mine, others):
        y = dot_full(rhs_top[t] - mine, linv[t + SUB])
        y_top[t] = y
        if t < TOP - 1:
            wait_linv(t + SUB)
            ylow[r, :HALF] = y.astype(BF16)
            ylow[1 - r, :HALF] = dot_split(rhs_top_other[t] - others, linv_other[t + SUB - 1]).astype(BF16)

    def forward_top(t):
        products(t + SUB, HALF)
        for i in ORDER:
            q = c ^ i
            value = share(t + SUB, q, HALF) + pend_top[q]
            send_ft[t + 1, q] = value.astype(BF16)
            for j in (1, 0):
                if i or j:
                    to((l, r ^ j, q), send_ft.at[t + 1, q], recv_ft.at[t, me], sf_sem.at[t + SUB], rf_sem.at[t + SUB + 1])
        recv_ft[t, me] = send_ft[t + 1, c]
        if t == 0:
            for q in range(COLS):
                pend_top[q] = share(t + SUB, COLS + q, HALF)

    wait_for(recv_5.at[pl.ds(0, 4 * COLS - 1)], rf_sem.at[SUB])

    def add_up_5(row):
        return add_up(recv_5.at[pl.ds(row * COLS, COLS)], HALF) + add_up(
            recv_5.at[pl.ds((2 + row) * COLS, COLS)], HALF
        )

    arrive_top(0, add_up_5(r), add_up_5(1 - r))
    forward_top(0)
    for t in (1, 2):
        wait_for(recv_ft.at[t - 1, pl.ds(0, 2 * COLS - 1)], rf_sem.at[t + SUB])
        mine = add_up(recv_ft.at[t - 1, pl.ds(r * COLS, COLS)], HALF)
        if t == 1:
            arrive_top(1, mine, add_up(recv_ft.at[t - 1, pl.ds((1 - r) * COLS, COLS)], HALF))
            forward_top(1)
        else:
            arrive_top(2, mine, None)

    x7 = dot_full(y_top[2], uinv[7])
    top_mine[2] = x7
    send_bt[2, 0] = x7.astype(BF16)
    for i in ORDER:
        if i:
            to((l, r, c ^ i), send_bt.at[2, 0], recv_7.at[c], sb_sem.at[7], rb_sem.at[7])
    recv_7[c] = send_bt[2, 0]
    upper_copy.wait_recv()
    wait_for(recv_7.at[pl.ds(0, COLS - 1)], rb_sem.at[7])
    x_top[pl.ds(COLS, COLS)] = recv_7[...]

    def down(t, load, src, row):
        total = None
        for k in range(SLOTS):
            value = dot(load(k), upper[t, k])
            taken = value * src[row, k].astype(F32)
            total = value if total is None else total + value
            second = taken if k == 0 else second + taken
        at_first = r == 0
        parts = (total - second, second)
        return jnp.where(at_first, parts[0], parts[1]), jnp.where(at_first, parts[1], parts[0])

    def parts_of(t, mine, others, y):
        a = dot_full(y - mine, uinv[t])
        b = -dot_split(others, uinv_other[t - 1])
        return a, b

    mine, others = down(6, lambda k: x_top[COLS + top_tgt[1, k] % COLS], top_src, 1)
    a, b = parts_of(6, mine, others, y_top[1])
    top_mine[1] = a
    send_bt[1, 0] = a.astype(BF16)
    send_bt[1, 1] = b.astype(BF16)
    for i in ORDER:
        to((l, 1 - r, c ^ i), send_bt.at[1, 1], recv_6.at[COLS + c], sb_sem.at[6], rb_sem.at[6])
        if i:
            to((l, r, c ^ i), send_bt.at[1, 0], recv_6.at[c], sb_sem.at[6], rb_sem.at[6])
    recv_6[c] = send_bt[1, 0]
    wait_for(recv_6.at[pl.ds(0, 2 * COLS - 1)], rb_sem.at[6])
    for q in range(COLS):
        x_top[q] = (recv_6[q].astype(F32) + recv_6[COLS + q].astype(F32)).astype(BF16)
    top_mine[1] = top_mine[1] + recv_6[COLS + c].astype(F32)
    six_out[...] = x_top[pl.ds(0, COLS)]
    x6_copy = to(other_core, six_out, six_in, misc_send.at[7], misc_recv.at[7])

    mine, others = down(5, lambda k: x_top[top_tgt[0, k]], top_src, 0)
    a, b = parts_of(5, mine, others, y_top[0])
    top_mine[0] = a
    send_bt[0, 0] = a.astype(BF16)
    send_bt[0, 1] = b.astype(BF16)
    slot_a = half * 2 * COLS + c
    for i in ORDER:
        for flip in (1, 0):
            to((l ^ flip, 1 - r, c ^ i), send_bt.at[0, 1], recv_b5.at[slot_a + COLS], sb_sem.at[5], rb_sem.at[5])
            if i or flip:
                to((l ^ flip, r, c ^ i), send_bt.at[0, 0], recv_b5.at[slot_a], sb_sem.at[5], rb_sem.at[5])
    recv_b5[slot_a] = send_bt[0, 0]
    x6_copy.wait_recv()
    for q in range(COLS):
        x_sub[6 * COLS + q, half] = x_top[q]
        x_sub[6 * COLS + q, 1 - half] = six_in[q]
    wait_for(recv_b5.at[pl.ds(0, 4 * COLS - 1)], rb_sem.at[5])
    for q in range(COLS):
        for h in range(2):
            x_sub[5 * COLS + q, h] = (
                recv_b5[h * 2 * COLS + q].astype(F32) + recv_b5[h * 2 * COLS + COLS + q].astype(F32)
            ).astype(BF16)
    top_mine[0] = top_mine[0] + recv_b5[slot_a + COLS].astype(F32)
    top_copy = to(other_core, top_mine, top_other, misc_send.at[8], misc_recv.at[8])

    def down_sub(t):
        return down(
            t,
            lambda k: x_sub[(t + 1) * COLS + sub_tgt[t, k]].reshape(SIDES, WIDTH),
            sub_src,
            t,
        )

    @pl.loop(0, SUB - 1)
    def _(step):
        t = SUB - 1 - step
        mine, others = down_sub(t)
        a, b = parts_of(t, mine, others, y_sub[t])
        send_b[t, 0] = a.astype(BF16)
        send_b[t, 1] = b.astype(BF16)
        for i in ORDER:
            to((l, 1 - r, c ^ i), send_b.at[t, 1], recv_b.at[t, COLS + c], sb_sem.at[t], rb_sem.at[t])
            if i:
                to((l, r, c ^ i), send_b.at[t, 0], recv_b.at[t, c], sb_sem.at[t], rb_sem.at[t])
        recv_b[t, c] = send_b[t, 0]
        wait_for(recv_b.at[t, pl.ds(0, 2 * COLS - 1)], rb_sem.at[t])
        for q in range(COLS):
            x = (recv_b[t, q].astype(F32) + recv_b[t, COLS + q].astype(F32)).astype(BF16)
            x_sub[t * COLS + q] = x.reshape(2, HALF, WIDTH)
        sub_out[t] = a + recv_b[t, COLS + c].astype(F32)

    mine, others = down_sub(0)
    last_out[...] = others
    last = to(other_row, last_out, last_in, misc_send.at[9], misc_recv.at[9])
    top_copy.wait_recv()
    for t in range(TOP):
        top_out[t, half_rows] = top_mine[t]
        top_out[t, pl.ds(pl.multiple_of((1 - half) * HALF, HALF), HALF)] = top_other[t]

    for copy in lin_copies + [rhs_copy, rhs_top_copy, *core_copies, six_copy, upper_copy, x6_copy, top_copy]:
        copy.wait_send()
    for t in range(SUB - 1):
        wait_for(recv_f.at[t, pl.ds(0, 2 * COLS - 1)], sf_sem.at[t])
    wait_for(recv_5.at[pl.ds(0, 4 * COLS - 1)], sf_sem.at[4])
    wait_for(recv_ft.at[0, pl.ds(0, 2 * COLS - 1)], sf_sem.at[5])
    wait_for(recv_ft.at[1, pl.ds(0, 2 * COLS - 1)], sf_sem.at[6])
    wait_for(recv_7.at[pl.ds(0, COLS - 1)], sb_sem.at[7])
    wait_for(recv_6.at[pl.ds(0, 2 * COLS - 1)], sb_sem.at[6])
    wait_for(recv_b5.at[pl.ds(0, 4 * COLS - 1)], sb_sem.at[5])
    for t in range(1, SUB):
        wait_for(recv_b.at[t, pl.ds(0, 2 * COLS - 1)], sb_sem.at[t])
    last.wait_send()
    last.wait_recv()
    sub_out[0] = dot_full(y_sub[0] - mine - last_in[...], uinv[0])


def local(*args):
    flat = [a.reshape(a.shape[3:] if i < 7 else a.shape[2:]) for i, a in enumerate(args)]
    vmem, smem, dma = pltpu.VMEM, pltpu.SMEM, pltpu.SemaphoreType.DMA
    tile = (SIDES, WIDTH)
    half = (HALF, WIDTH)
    block = (WIDTH, WIDTH)
    scratch = [
        vmem((LINKED, SLOTS) + block, BF16),
        vmem((LINKED, SLOTS) + block, BF16),
        vmem((SUB + TOP,) + block, F32),
        vmem((SUB + TOP,) + block, F32),
        vmem((SUB,) + tile, F32),
        vmem((TOP,) + half, F32),
        vmem((6,) + block, BF16),
        vmem((6,) + block, BF16),
        vmem((6,) + block, BF16),
        vmem((6,) + block, BF16),
        vmem((SUB - 1,) + tile, F32),
        vmem((2,) + half, F32),
        smem((LINKED, SLOTS), jnp.int32),
        smem((LINKED, SLOTS), jnp.int32),
        smem((LINKED, 2 * COLS + 1), jnp.int32),
        vmem((2,) + tile, BF16),
        vmem(tile, BF16),
        vmem((SUB,) + tile, F32),
        vmem((TOP,) + half, F32),
        vmem((SLOTS + 1,) + tile, F32),
        vmem((COLS,) + tile, F32),
        vmem((COLS,) + half, F32),
        vmem((SUB - 1, COLS) + tile, BF16),
        vmem((SUB - 1, 2 * COLS) + tile, BF16),
        vmem((TOP, COLS) + half, BF16),
        vmem((4 * COLS,) + half, BF16),
        vmem((2, 2 * COLS) + half, BF16),
        vmem((2, 2, COLS) + half, F32),
        vmem((2, COLS) + half, BF16),
        vmem((2, COLS) + half, BF16),
        vmem((2, COLS) + half, BF16),
        vmem((7 * COLS, 2) + half, BF16),
        vmem((2 * COLS,) + half, BF16),
        vmem((SUB, 2) + tile, BF16),
        vmem((SUB, 2 * COLS) + tile, BF16),
        vmem((TOP, 2) + half, BF16),
        vmem((COLS,) + half, BF16),
        vmem((2 * COLS,) + half, BF16),
        vmem((4 * COLS,) + half, BF16),
        vmem((COLS,) + half, BF16),
        vmem((COLS,) + half, BF16),
        vmem(tile, F32),
        vmem(tile, F32),
        vmem((TOP,) + half, F32),
        vmem((TOP,) + half, F32),
        dma((10,)),
        dma((2, 6)),
        dma((10,)),
        dma((10,)),
        dma((SUB + TOP,)),
        dma((SUB + TOP,)),
        dma((SUB + TOP,)),
        dma((SUB + TOP,)),
    ]
    any_spec = pl.BlockSpec(memory_space=pl.ANY)
    smem_spec = pl.BlockSpec(memory_space=pltpu.SMEM)
    vmem_spec = pl.BlockSpec(memory_space=pltpu.VMEM)
    sub, top = pl.pallas_call(
        kernel,
        out_shape=(
            jax.ShapeDtypeStruct((SUB,) + tile, F32),
            jax.ShapeDtypeStruct((TOP,) + tile, F32),
        ),
        in_specs=([any_spec] * 5 + [smem_spec] * 2) * 2,
        out_specs=(vmem_spec, vmem_spec),
        scratch_shapes=scratch,
        compiler_params=pltpu.CompilerParams(
            collective_id=0, has_side_effects=True, vmem_limit_bytes=40 * 1024 * 1024
        ),
    )(*flat)
    return sub[None, None, None], top[None, None]


def solution(mesh):
    sub = P("layer", "prow", "pcol")
    top = P("prow", "pcol")
    return jax.shard_map(
        local, mesh=mesh, in_specs=(sub,) * 7 + (top,) * 7, out_specs=(sub, top), check_vma=False
    )
```

```python
import jax
import jax.numpy as jnp
from jax import lax
from jax.experimental import pallas as pl
from jax.experimental.pallas import tpu as pltpu
from jax.sharding import PartitionSpec as P

MESH = pl.DeviceIdType.MESH
F32 = jnp.float32
BF16 = jnp.bfloat16
SUB, TOP, SLOTS, COLS, SIDES, WIDTH = 5, 3, 16, 16, 32, 128
HALF = SIDES // 2
LINKED = SUB + TOP - 1
ORDER = (10, 9, 11, 6, 14, 5, 7, 13, 15, 8, 2, 1, 3, 4, 12, 0)


def dot(a, b):
    return jnp.dot(a, b, preferred_element_type=F32)


def dot_full(a, b):
    return jnp.dot(a, b, preferred_element_type=F32, precision=lax.Precision.HIGHEST)


def dot_split(a, b):
    high = a.astype(BF16)
    low = (a - high.astype(F32)).astype(BF16)
    return dot(high, b) + dot(low, b)


def wait_for(ref, sem):
    pltpu.make_async_copy(ref, ref, sem).wait()


def kernel(
    sub_rhs, sub_linv, sub_uinv, sub_lower, sub_upper, sub_src_in, sub_tgt_in,
    top_rhs, top_linv, top_uinv, top_lower, top_upper, top_src_in, top_tgt_in,
    sub_out, top_out,
    sub_src, sub_tgt, top_src, top_tgt,
    lower, upper, linv, uinv, rhs_sub, rhs_top,
    linv_low, uinv_low, linv_other, uinv_other, rhs_sub_other, rhs_top_other,
    perm, psrc, ends,
    ylow, ylow_other, y_sub, y_top, sums, pend, pend_top,
    send_f, recv_f, send_ft, recv_5, recv_ft,
    halves, core_out, core_in, six,
    x_sub, x_top, send_b, recv_b, send_bt, recv_7, recv_6, recv_b5, six_in, six_out, last_out, last_in, top_mine, top_other,
    load_sem, lin_sem, group_sem, misc_recv, misc_send, rf_sem, sf_sem, rb_sem, sb_sem,
):
    l, r, c = lax.axis_index("layer"), lax.axis_index("prow"), lax.axis_index("pcol")
    high, half = l // 2, l % 2
    half_rows = pl.ds(pl.multiple_of(half * HALF, HALF), HALF)
    me = r * COLS + c

    loads = (
        (sub_lower, lower.at[pl.ds(0, SUB)]),
        (top_lower, lower.at[pl.ds(SUB, TOP - 1)]),
        (sub_upper, upper.at[pl.ds(0, SUB)]),
        (top_upper, upper.at[pl.ds(SUB, TOP - 1)]),
        (sub_linv, linv.at[pl.ds(0, SUB)]),
        (top_linv, linv.at[pl.ds(SUB, TOP)]),
        (sub_uinv, uinv.at[pl.ds(0, SUB)]),
        (top_uinv, uinv.at[pl.ds(SUB, TOP)]),
        (sub_rhs, rhs_sub),
        (top_rhs.at[:, half_rows], rhs_top),
        (sub_src_in, sub_src),
        (sub_tgt_in, sub_tgt),
        (top_src_in, top_src),
        (top_tgt_in, top_tgt),
    )
    copies = [pltpu.make_async_copy(a, b, load_sem.at[i]) for i, (a, b) in enumerate(loads)]
    for i in (8, 4, 10, 11, 12, 13, 0, 5, 9, 6, 7, 1, 2, 3):
        copies[i].start()

    barrier = pltpu.get_barrier_semaphore()
    for flip in (1, 2):
        pl.semaphore_signal(barrier, inc=1, device_id=(l ^ flip, r, c), device_id_type=MESH)
    for i in ORDER:
        for j in (1, 0):
            if j or i:
                pl.semaphore_signal(barrier, inc=1, device_id=(l, r ^ j, c ^ i), device_id_type=MESH)

    def sort_level(src, tgt, row, t):
        codes = [tgt[(*row, k)] for k in range(SLOTS)]
        rank = [jnp.int32(0)] * SLOTS
        for k in range(SLOTS):
            for j in range(k):
                before = (codes[j] <= codes[k]).astype(jnp.int32)
                rank[k] = rank[k] + before
                rank[j] = rank[j] + (1 - before)
        for i in range(SLOTS):
            slot = jnp.int32(0)
            for k in range(1, SLOTS):
                slot = slot + jnp.where(rank[k] == i, k, 0)
            perm[t, i] = slot
            psrc[t, i] = src[(*row, slot)]
        ends[t, 0] = 0
        for q in range(2 * COLS):
            count = jnp.int32(0)
            for k in range(SLOTS):
                count = count + (codes[k] <= q).astype(jnp.int32)
            ends[t, q + 1] = count

    copies[8].wait()
    copies[4].wait()
    y0 = dot_full(rhs_sub[0], linv[0])
    y_sub[0] = y0
    ylow[r] = y0.astype(BF16)
    pl.semaphore_wait(barrier, 33)

    def to(device, src, dst, send_sem, recv_sem):
        copy = pltpu.make_async_remote_copy(
            src_ref=src, dst_ref=dst, send_sem=send_sem, recv_sem=recv_sem, device_id=device, device_id_type=MESH
        )
        copy.start()
        return copy

    other_row = (l, 1 - r, c)
    other_core = (l ^ 1, r, c)
    other_high = (l ^ 2, r, c)

    first = to(other_row, ylow.at[r], ylow_other, misc_send.at[0], misc_recv.at[0])
    copies[10].wait()
    copies[11].wait()
    sort_level(sub_src, sub_tgt, (0, 0), 0)
    for i in (5, 6, 7, 9, 0, 1, 2, 3, 12, 13):
        copies[i].wait()

    def lin_copy(t):
        linv_low[t - 1] = linv[t].astype(BF16)
        return to(other_row, linv_low.at[t - 1], linv_other.at[t - 1], lin_sem.at[0, t - 1], lin_sem.at[1, t - 1])

    def uin_copy(t):
        uinv_low[t - 1] = uinv[t].astype(BF16)
        return to(other_row, uinv_low.at[t - 1], uinv_other.at[t - 1], lin_sem.at[2, t - 1], lin_sem.at[3, t - 1])

    def rhs_copy(t):
        return to(other_row, rhs_sub.at[t], rhs_sub_other.at[t - 1], lin_sem.at[4, t - 1], lin_sem.at[5, t - 1])

    def rhs_top_copy(t):
        return to(other_row, rhs_top.at[t], rhs_top_other.at[t], lin_sem.at[4, t + 4], lin_sem.at[5, t + 4])

    for t in (1, 2):
        lin_copy(t)
        rhs_copy(t)

    def wait_linv(t):
        wait_for(linv_other.at[t - 1], lin_sem.at[1, t - 1])

    def products(t, rows):
        total = jnp.zeros((rows, WIDTH), F32)
        sums[0, :rows] = total
        for i in range(SLOTS):
            value = ylow[psrc[t, i]]
            total = total + dot(value[:rows], lower[t, perm[t, i]])
            sums[i + 1, :rows] = total

    def share(t, code, rows):
        return sums[ends[t, code + 1], :rows] - sums[ends[t, code], :rows]

    def forward(t):
        products(t, SIDES)
        for i in ORDER:
            q = c ^ i
            send_f[t, q] = (share(t, q, SIDES) + pend[q]).astype(BF16)
            for j in (1, 0):
                if i or j:
                    to((l, r ^ j, q), send_f.at[t, q], recv_f.at[t, me], sf_sem.at[t], rf_sem.at[t + 1])
        recv_f[t, me] = send_f[t, c]
        for q in range(COLS):
            pend[q] = share(t, COLS + q, SIDES)

    def add_up(ref, rows):
        parts = [ref[i].astype(F32) for i in range(COLS)]
        while len(parts) > 1:
            parts = [a + b for a, b in zip(parts[::2], parts[1::2])]
        return parts[0]

    def arrive(t):
        wait_for(recv_f.at[t - 1, pl.ds(0, 2 * COLS - 1)], rf_sem.at[t])
        wait_linv(t)
        wait_for(rhs_sub_other.at[t - 1], lin_sem.at[5, t - 1])
        mine = rhs_sub[t] - add_up(recv_f.at[t - 1, pl.ds(r * COLS, COLS)], SIDES)
        others = rhs_sub_other[t - 1] - add_up(recv_f.at[t - 1, pl.ds((1 - r) * COLS, COLS)], SIDES)
        y = dot_full(mine, linv[t])
        y_sub[t] = y
        ylow[r] = y.astype(BF16)
        ylow[1 - r] = dot_split(others, linv_other[t - 1]).astype(BF16)

    first.wait_recv()
    first.wait_send()
    ylow[1 - r] = ylow_other[...]

    @pl.loop(0, COLS)
    def _(q):
        pend[q] = jnp.zeros((SIDES, WIDTH), F32)

    forward(0)
    sort_level(sub_src, sub_tgt, (1, 0), 1)
    arrive(1)
    for flip in (1, 2):
        pl.semaphore_signal(group_sem.at[flip - 1], inc=1, device_id=(l ^ flip, r, c), device_id_type=MESH)
    forward(1)
    lin_copy(3)
    rhs_copy(3)
    sort_level(sub_src, sub_tgt, (2, 0), 2)

    @pl.loop(2, SUB - 1)
    def _(t):
        arrive(t)
        forward(t)
        lin_copy(t + 2)

        @pl.when(t == 2)
        def _():
            rhs_copy(t + 2)

        @pl.when(t == 3)
        def _():
            rhs_top_copy(0)
            rhs_top_copy(1)

        sort_level(sub_src, sub_tgt, (t + 1, 0), t + 1)

    t = SUB - 1
    arrive(t)
    products(t, SIDES)
    for q in range(COLS):
        both = share(t, q, SIDES) + pend[q]
        halves[0, 0, q] = both[:HALF]
        halves[0, 1, q] = both[HALF:]
    core_out[0] = halves[0, 1 - half].astype(BF16)
    core_copies = [to(other_core, core_out.at[0], core_in.at[0], misc_send.at[3], misc_recv.at[3])]
    for q in range(COLS):
        both = share(t, COLS + q, SIDES)
        halves[1, 0, q] = both[:HALF]
        halves[1, 1, q] = both[HALF:]
    core_out[1] = halves[1, 1 - half].astype(BF16)
    core_copies.append(to(other_core, core_out.at[1], core_in.at[1], misc_send.at[4], misc_recv.at[4]))
    core_copies[0].wait_recv()
    pl.semaphore_wait(group_sem.at[1], 1)
    slot_5 = high * 2 * COLS + me
    for i in ORDER:
        q = c ^ i
        send_ft[0, q] = (halves[0, half, q] + core_in[0, q].astype(F32)).astype(BF16)
        for flip in (2, 0):
            for j in (1, 0):
                if i or j or flip:
                    to((l ^ flip, r ^ j, q), send_ft.at[0, q], recv_5.at[slot_5], sf_sem.at[t], rf_sem.at[t + 1])
    recv_5[slot_5] = send_ft[0, c]
    lin_copy(6)
    core_copies[1].wait_recv()
    six[high] = (halves[1, half] + core_in[1].astype(F32)).astype(BF16)
    six_copy = to(other_high, six.at[high], six.at[high], misc_send.at[5], misc_recv.at[5])
    for t in (6, 5):
        uin_copy(t)
    sort_level(top_src, top_tgt, (0,), SUB)
    sort_level(top_src, top_tgt, (1,), SUB + 1)
    six_copy.wait_recv()
    for q in range(COLS):
        pend_top[q] = six[0, q].astype(F32) + six[1, q].astype(F32)

    def arrive_top(t, mine, others):
        y = dot_full(rhs_top[t] - mine, linv[t + SUB])
        y_top[t] = y
        if t < TOP - 1:
            wait_linv(t + SUB)
            wait_for(rhs_top_other.at[t], lin_sem.at[5, t + 4])
            ylow[r, :HALF] = y.astype(BF16)
            ylow[1 - r, :HALF] = dot_split(rhs_top_other[t] - others, linv_other[t + SUB - 1]).astype(BF16)

    def forward_top(t):
        products(t + SUB, HALF)
        for i in ORDER:
            q = c ^ i
            value = share(t + SUB, q, HALF) + pend_top[q]
            send_ft[t + 1, q] = value.astype(BF16)
            for j in (1, 0):
                if i or j:
                    to((l, r ^ j, q), send_ft.at[t + 1, q], recv_ft.at[t, me], sf_sem.at[t + SUB], rf_sem.at[t + SUB + 1])
        recv_ft[t, me] = send_ft[t + 1, c]
        for u in (4 - 2 * t, 3 - 2 * t):
            uin_copy(u)
        if t == 0:
            for q in range(COLS):
                pend_top[q] = share(t + SUB, COLS + q, HALF)

    wait_for(recv_5.at[pl.ds(0, 4 * COLS - 1)], rf_sem.at[SUB])

    def add_up_5(row):
        return add_up(recv_5.at[pl.ds(row * COLS, COLS)], HALF) + add_up(
            recv_5.at[pl.ds((2 + row) * COLS, COLS)], HALF
        )

    arrive_top(0, add_up_5(r), add_up_5(1 - r))
    forward_top(0)
    for t in (1, 2):
        wait_for(recv_ft.at[t - 1, pl.ds(0, 2 * COLS - 1)], rf_sem.at[t + SUB])
        mine = add_up(recv_ft.at[t - 1, pl.ds(r * COLS, COLS)], HALF)
        if t == 1:
            arrive_top(1, mine, add_up(recv_ft.at[t - 1, pl.ds((1 - r) * COLS, COLS)], HALF))
            forward_top(1)
        else:
            arrive_top(2, mine, None)

    x7 = dot_full(y_top[2], uinv[7])
    top_mine[2] = x7
    send_bt[2, 0] = x7.astype(BF16)
    for i in ORDER:
        if i:
            to((l, r, c ^ i), send_bt.at[2, 0], recv_7.at[c], sb_sem.at[7], rb_sem.at[7])
    recv_7[c] = send_bt[2, 0]
    wait_for(recv_7.at[pl.ds(0, COLS - 1)], rb_sem.at[7])
    x_top[pl.ds(COLS, COLS)] = recv_7[...]

    def down(t, load, src, row):
        total = None
        for k in range(SLOTS):
            value = dot(load(k), upper[t, k])
            taken = value * src[(*row, k)].astype(F32)
            total = value if total is None else total + value
            second = taken if k == 0 else second + taken
        at_first = r == 0
        parts = (total - second, second)
        return jnp.where(at_first, parts[0], parts[1]), jnp.where(at_first, parts[1], parts[0])

    def parts_of(t, mine, others, y):
        a = dot_full(y - mine, uinv[t])
        wait_for(uinv_other.at[t - 1], lin_sem.at[3, t - 1])
        b = -dot_split(others, uinv_other[t - 1])
        return a, b

    mine, others = down(6, lambda k: x_top[COLS + top_tgt[1, k] % COLS], top_src, (1,))
    a, b = parts_of(6, mine, others, y_top[1])
    top_mine[1] = a
    send_bt[1, 0] = a.astype(BF16)
    send_bt[1, 1] = b.astype(BF16)
    for i in ORDER:
        to((l, 1 - r, c ^ i), send_bt.at[1, 1], recv_6.at[COLS + c], sb_sem.at[6], rb_sem.at[6])
        if i:
            to((l, r, c ^ i), send_bt.at[1, 0], recv_6.at[c], sb_sem.at[6], rb_sem.at[6])
    recv_6[c] = send_bt[1, 0]
    wait_for(recv_6.at[pl.ds(0, 2 * COLS - 1)], rb_sem.at[6])
    for q in range(COLS):
        x_top[q] = (recv_6[q].astype(F32) + recv_6[COLS + q].astype(F32)).astype(BF16)
    top_mine[1] = top_mine[1] + recv_6[COLS + c].astype(F32)
    six_out[...] = x_top[pl.ds(0, COLS)]
    x6_copy = to(other_core, six_out, six_in, misc_send.at[7], misc_recv.at[7])

    mine, others = down(5, lambda k: x_top[top_tgt[0, k]], top_src, (0,))
    a, b = parts_of(5, mine, others, y_top[0])
    top_mine[0] = a
    send_bt[0, 0] = a.astype(BF16)
    send_bt[0, 1] = b.astype(BF16)
    pl.semaphore_wait(group_sem.at[0], 1)
    slot_a = half * 2 * COLS + c
    for i in ORDER:
        for flip in (1, 0):
            to((l ^ flip, 1 - r, c ^ i), send_bt.at[0, 1], recv_b5.at[slot_a + COLS], sb_sem.at[5], rb_sem.at[5])
            if i or flip:
                to((l ^ flip, r, c ^ i), send_bt.at[0, 0], recv_b5.at[slot_a], sb_sem.at[5], rb_sem.at[5])
    recv_b5[slot_a] = send_bt[0, 0]
    x6_copy.wait_recv()
    for q in range(COLS):
        x_sub[6 * COLS + q, half] = x_top[q]
        x_sub[6 * COLS + q, 1 - half] = six_in[q]
    wait_for(recv_b5.at[pl.ds(0, 4 * COLS - 1)], rb_sem.at[5])
    for q in range(COLS):
        for h in range(2):
            x_sub[5 * COLS + q, h] = (
                recv_b5[h * 2 * COLS + q].astype(F32) + recv_b5[h * 2 * COLS + COLS + q].astype(F32)
            ).astype(BF16)
    top_mine[0] = top_mine[0] + recv_b5[slot_a + COLS].astype(F32)
    top_copy = to(other_core, top_mine, top_other, misc_send.at[8], misc_recv.at[8])

    def down_sub(t):
        return down(
            t,
            lambda k: x_sub[(t + 1) * COLS + sub_tgt[t, 0, k]].reshape(SIDES, WIDTH),
            sub_src,
            (t, 0),
        )

    @pl.loop(0, SUB - 1)
    def _(step):
        t = SUB - 1 - step
        mine, others = down_sub(t)
        a, b = parts_of(t, mine, others, y_sub[t])
        send_b[t, 0] = a.astype(BF16)
        send_b[t, 1] = b.astype(BF16)
        for i in ORDER:
            to((l, 1 - r, c ^ i), send_b.at[t, 1], recv_b.at[t, COLS + c], sb_sem.at[t], rb_sem.at[t])
            if i:
                to((l, r, c ^ i), send_b.at[t, 0], recv_b.at[t, c], sb_sem.at[t], rb_sem.at[t])
        recv_b[t, c] = send_b[t, 0]
        wait_for(recv_b.at[t, pl.ds(0, 2 * COLS - 1)], rb_sem.at[t])
        for q in range(COLS):
            x = (recv_b[t, q].astype(F32) + recv_b[t, COLS + q].astype(F32)).astype(BF16)
            x_sub[t * COLS + q] = x.reshape(2, HALF, WIDTH)
        sub_out[t] = a + recv_b[t, COLS + c].astype(F32)

    mine, others = down_sub(0)
    last_out[...] = others
    last = to(other_row, last_out, last_in, misc_send.at[9], misc_recv.at[9])
    top_copy.wait_recv()
    for t in range(TOP):
        top_out[t, half_rows] = top_mine[t]
        top_out[t, pl.ds(pl.multiple_of((1 - half) * HALF, HALF), HALF)] = top_other[t]

    for copy in (*core_copies, six_copy, x6_copy, top_copy):
        copy.wait_send()
    for t in range(6):
        wait_for(linv_other.at[t], lin_sem.at[0, t])
        wait_for(uinv_other.at[t], lin_sem.at[2, t])
        wait_for(rhs_sub_other.at[t] if t < 4 else rhs_top_other.at[t - 4], lin_sem.at[4, t])
    for t in range(SUB - 1):
        wait_for(recv_f.at[t, pl.ds(0, 2 * COLS - 1)], sf_sem.at[t])
    wait_for(recv_5.at[pl.ds(0, 4 * COLS - 1)], sf_sem.at[4])
    wait_for(recv_ft.at[0, pl.ds(0, 2 * COLS - 1)], sf_sem.at[5])
    wait_for(recv_ft.at[1, pl.ds(0, 2 * COLS - 1)], sf_sem.at[6])
    wait_for(recv_7.at[pl.ds(0, COLS - 1)], sb_sem.at[7])
    wait_for(recv_6.at[pl.ds(0, 2 * COLS - 1)], sb_sem.at[6])
    wait_for(recv_b5.at[pl.ds(0, 4 * COLS - 1)], sb_sem.at[5])
    for t in range(1, SUB):
        wait_for(recv_b.at[t, pl.ds(0, 2 * COLS - 1)], sb_sem.at[t])
    last.wait_send()
    last.wait_recv()
    sub_out[0] = dot_full(y_sub[0] - mine - last_in[...], uinv[0])


def hand_over(sub, top):
    def body(sub_in, top_in, sub_res, top_res):
        sub_res[0, 0, 0] = sub_in[...]
        top_res[0, 0] = top_in[...]

    vmem_spec = pl.BlockSpec(memory_space=pltpu.VMEM)
    return pl.pallas_call(
        body,
        out_shape=(
            jax.ShapeDtypeStruct((1, 1, 1) + sub.shape, F32),
            jax.ShapeDtypeStruct((1, 1) + top.shape, F32),
        ),
        in_specs=[vmem_spec] * 2,
        out_specs=[vmem_spec] * 2,
    )(sub, top)


def local(*args):
    flat = [a.reshape(a.shape[3:] if i < 7 else a.shape[2:]) for i, a in enumerate(args)]
    flat[5], flat[6] = (a.reshape(SUB, 1, SLOTS) for a in args[5:7])
    vmem, smem, dma = pltpu.VMEM, pltpu.SMEM, pltpu.SemaphoreType.DMA
    tile = (SIDES, WIDTH)
    half = (HALF, WIDTH)
    block = (WIDTH, WIDTH)
    scratch = [
        smem((SUB, 1, SLOTS), jnp.int32),
        smem((SUB, 1, SLOTS), jnp.int32),
        smem((TOP - 1, SLOTS), jnp.int32),
        smem((TOP - 1, SLOTS), jnp.int32),
        vmem((LINKED, SLOTS) + block, BF16),
        vmem((LINKED, SLOTS) + block, BF16),
        vmem((SUB + TOP,) + block, F32),
        vmem((SUB + TOP,) + block, F32),
        vmem((SUB,) + tile, F32),
        vmem((TOP,) + half, F32),
        vmem((6,) + block, BF16),
        vmem((6,) + block, BF16),
        vmem((6,) + block, BF16),
        vmem((6,) + block, BF16),
        vmem((SUB - 1,) + tile, F32),
        vmem((2,) + half, F32),
        smem((LINKED, SLOTS), jnp.int32),
        smem((LINKED, SLOTS), jnp.int32),
        smem((LINKED, 2 * COLS + 1), jnp.int32),
        vmem((2,) + tile, BF16),
        vmem(tile, BF16),
        vmem((SUB,) + tile, F32),
        vmem((TOP,) + half, F32),
        vmem((SLOTS + 1,) + tile, F32),
        vmem((COLS,) + tile, F32),
        vmem((COLS,) + half, F32),
        vmem((SUB - 1, COLS) + tile, BF16),
        vmem((SUB - 1, 2 * COLS) + tile, BF16),
        vmem((TOP, COLS) + half, BF16),
        vmem((4 * COLS,) + half, BF16),
        vmem((2, 2 * COLS) + half, BF16),
        vmem((2, 2, COLS) + half, F32),
        vmem((2, COLS) + half, BF16),
        vmem((2, COLS) + half, BF16),
        vmem((2, COLS) + half, BF16),
        vmem((7 * COLS, 2) + half, BF16),
        vmem((2 * COLS,) + half, BF16),
        vmem((SUB, 2) + tile, BF16),
        vmem((SUB, 2 * COLS) + tile, BF16),
        vmem((TOP, 2) + half, BF16),
        vmem((COLS,) + half, BF16),
        vmem((2 * COLS,) + half, BF16),
        vmem((4 * COLS,) + half, BF16),
        vmem((COLS,) + half, BF16),
        vmem((COLS,) + half, BF16),
        vmem(tile, F32),
        vmem(tile, F32),
        vmem((TOP,) + half, F32),
        vmem((TOP,) + half, F32),
        dma((14,)),
        dma((6, 6)),
        pltpu.SemaphoreType.REGULAR((2,)),
        dma((10,)),
        dma((10,)),
        dma((SUB + TOP,)),
        dma((SUB + TOP,)),
        dma((SUB + TOP,)),
        dma((SUB + TOP,)),
    ]
    any_spec = pl.BlockSpec(memory_space=pl.ANY)
    vmem_spec = pl.BlockSpec(memory_space=pltpu.VMEM)
    sub, top = pl.pallas_call(
        kernel,
        out_shape=(
            jax.ShapeDtypeStruct((SUB,) + tile, F32),
            jax.ShapeDtypeStruct((TOP,) + tile, F32),
        ),
        in_specs=[any_spec] * 14,
        out_specs=(vmem_spec, vmem_spec),
        scratch_shapes=scratch,
        compiler_params=pltpu.CompilerParams(
            collective_id=0, has_side_effects=True, vmem_limit_bytes=60 * 1024 * 1024
        ),
    )(*flat)
    return hand_over(sub, top)


def solution(mesh):
    sub = P("layer", "prow", "pcol")
    top = P("prow", "pcol")
    return jax.shard_map(
        local, mesh=mesh, in_specs=(sub,) * 7 + (top,) * 7, out_specs=(sub, top), check_vma=False
    )
```

```python
import jax
import jax.numpy as jnp
from jax import lax
from jax.experimental import pallas as pl
from jax.experimental.pallas import tpu as pltpu
from jax.sharding import PartitionSpec as P

MESH = pl.DeviceIdType.MESH
F32 = jnp.float32
BF16 = jnp.bfloat16
SUB, TOP, SLOTS, COLS, SIDES, WIDTH = 5, 3, 16, 16, 32, 128
HALF = SIDES // 2
LINKED = SUB + TOP - 1
ORDER = (10, 9, 11, 6, 14, 5, 7, 13, 15, 8, 2, 1, 3, 4, 12, 0)


def dot(a, b):
    return jnp.dot(a, b, preferred_element_type=F32)


def dot_full(a, b):
    return jnp.dot(a, b, preferred_element_type=F32, precision=lax.Precision.HIGHEST)


def dot_split(a, b):
    high = a.astype(BF16)
    low = (a - high.astype(F32)).astype(BF16)
    return dot(high, b) + dot(low, b)


def wait_for(ref, sem):
    pltpu.make_async_copy(ref, ref, sem).wait()


def kernel(
    sub_rhs, sub_linv, sub_uinv, sub_lower, sub_upper, sub_src_in, sub_tgt_in,
    top_rhs, top_linv, top_uinv, top_lower, top_upper, top_src_in, top_tgt_in,
    sub_out, top_out,
    sub_src, sub_tgt, top_src, top_tgt,
    lower_0, lower, upper, linv, uinv, rhs_sub, rhs_top,
    linv_low, uinv_low, linv_other, uinv_other, rhs_sub_other, rhs_top_other,
    perm, psrc, ends,
    ylow, ylow_swap, y_sub, y_top, sums, pend, pend_top,
    send_f, recv_f, send_ft, recv_5, recv_ft,
    halves, core_out, core_in, six,
    x_sub, x_top, send_b, recv_b, send_bt, recv_7, recv_6, recv_b5, six_in, six_out, last_out, last_in, top_mine, top_other,
    both_low, load_sem, lin_sem, group_sem, misc_recv, misc_send, rf_sem, sf_sem, rb_sem, sb_sem,
):
    l, r, c = lax.axis_index("layer"), lax.axis_index("prow"), lax.axis_index("pcol")
    high, half = l // 2, l % 2
    half_rows = pl.ds(pl.multiple_of(half * HALF, HALF), HALF)
    me = r * COLS + c

    loads = (
        (sub_lower.at[pl.ds(1, SUB - 1)], lower.at[pl.ds(1, SUB - 1)]),
        (top_lower, lower.at[pl.ds(SUB, TOP - 1)]),
        (sub_upper, upper.at[pl.ds(0, SUB)]),
        (top_upper, upper.at[pl.ds(SUB, TOP - 1)]),
        (sub_linv, linv.at[pl.ds(0, SUB)]),
        (top_linv, linv.at[pl.ds(SUB, TOP)]),
        (sub_uinv, uinv.at[pl.ds(0, SUB)]),
        (top_uinv, uinv.at[pl.ds(SUB, TOP)]),
        (sub_rhs, rhs_sub),
        (top_rhs.at[:, half_rows], rhs_top),
        (sub_src_in, sub_src),
        (sub_tgt_in, sub_tgt),
        (top_src_in, top_src),
        (top_tgt_in, top_tgt),
        (sub_lower.at[0], lower_0),
    )
    copies = [pltpu.make_async_copy(a, b, load_sem.at[i]) for i, (a, b) in enumerate(loads)]
    for i in (8, 4, 10, 11, 14, 9, 5, 12, 13, 6, 7, 0, 1, 2, 3):
        copies[i].start()

    barrier = pltpu.get_barrier_semaphore()
    for flip in (1, 2):
        pl.semaphore_signal(barrier, inc=1, device_id=(l ^ flip, r, c), device_id_type=MESH)
    pl.semaphore_signal(barrier, inc=1, device_id=(l, 1 - r, c), device_id_type=MESH)
    for i in (1, 2, 3, 4, 8, 12):
        pl.semaphore_signal(barrier, inc=1, device_id=(l, r, c ^ i), device_id_type=MESH)

    def sort_level(src, tgt, row, t):
        codes = [tgt[(*row, k)] for k in range(SLOTS)]
        rank = [jnp.int32(0)] * SLOTS
        for k in range(SLOTS):
            for j in range(k):
                before = (codes[j] <= codes[k]).astype(jnp.int32)
                rank[k] = rank[k] + before
                rank[j] = rank[j] + (1 - before)
        for i in range(SLOTS):
            slot = jnp.int32(0)
            for k in range(1, SLOTS):
                slot = slot + jnp.where(rank[k] == i, k, 0)
            perm[t, i] = slot
            psrc[t, i] = src[(*row, slot)]
        ends[t, 0] = 0
        for q in range(2 * COLS):
            count = jnp.int32(0)
            for k in range(SLOTS):
                count = count + (codes[k] <= q).astype(jnp.int32)
            ends[t, q + 1] = count

    copies[8].wait()
    copies[4].wait()
    y0 = dot_full(rhs_sub[0].reshape(SIDES, WIDTH), linv[0]).reshape(2, HALF, WIDTH)
    y_sub[0] = y0
    ylow_swap[0] = y0.astype(BF16)
    for h in range(2):
        ylow[h, r] = ylow_swap[0, h]
    pl.semaphore_wait(barrier, 9)

    def to(device, src, dst, send_sem, recv_sem):
        copy = pltpu.make_async_remote_copy(
            src_ref=src, dst_ref=dst, send_sem=send_sem, recv_sem=recv_sem, device_id=device, device_id_type=MESH
        )
        copy.start()
        return copy

    other_row = (l, 1 - r, c)
    other_core = (l ^ 1, r, c)
    other_high = (l ^ 2, r, c)

    first = to(other_row, ylow_swap.at[0], ylow_swap.at[1], misc_send.at[0], misc_recv.at[0])
    for i in (4, 8, 12):
        pl.semaphore_signal(group_sem.at[2], inc=1, device_id=(l, r, c ^ i), device_id_type=MESH)
    copies[10].wait()
    copies[11].wait()
    sort_level(sub_src, sub_tgt, (0, 0), 0)

    def lin_copy(t):
        linv_low[t - 1] = linv[t].astype(BF16)
        return to(other_row, linv_low.at[t - 1], linv_other.at[t - 1], lin_sem.at[0, t - 1], lin_sem.at[1, t - 1])

    def uin_copy(t):
        uinv_low[t - 1] = uinv[t].astype(BF16)
        return to(other_row, uinv_low.at[t - 1], uinv_other.at[t - 1], lin_sem.at[2, t - 1], lin_sem.at[3, t - 1])

    def rhs_copy(t):
        return to(other_row, rhs_sub.at[t], rhs_sub_other.at[t - 1], lin_sem.at[4, t - 1], lin_sem.at[5, t - 1])

    def rhs_top_copy(t):
        return to(other_row, rhs_top.at[t], rhs_top_other.at[t], lin_sem.at[4, t + 4], lin_sem.at[5, t + 4])

    pl.semaphore_wait(group_sem.at[2], 3)
    pl.semaphore_signal(group_sem.at[3], inc=1, device_id=other_row, device_id_type=MESH)
    for t in (1, 2):
        lin_copy(t)
        rhs_copy(t)
    copies[14].wait()

    def wait_linv(t):
        wait_for(linv_other.at[t - 1], lin_sem.at[1, t - 1])

    streams = (1 - half, half)

    def products(h, t, block):
        total = jnp.zeros((HALF, WIDTH), F32)
        sums[h, 0] = total
        for i in range(SLOTS):
            total = total + dot(ylow[h, psrc[t, i]], block(perm[t, i]))
            sums[h, i + 1] = total

    def share(h, t, code):
        return sums[h, ends[t, code + 1]] - sums[h, ends[t, code]]

    def forward(h, t, block=None):
        products(h, t, block or (lambda k: lower[t, k]))
        for i in ORDER:
            q = c ^ i
            send_f[h, t, q] = (share(h, t, q) + pend[h, q]).astype(BF16)
            for j in (1, 0):
                if i or j:
                    to((l, r ^ j, q), send_f.at[h, t, q], recv_f.at[h, t, me], sf_sem.at[h, t], rf_sem.at[h, t + 1])
        recv_f[h, t, me] = send_f[h, t, c]

    def keep(h, t):
        for q in range(COLS):
            pend[h, q] = share(h, t, COLS + q)

    def add_up(ref, rows):
        parts = [ref[i].astype(F32) for i in range(COLS)]
        while len(parts) > 1:
            parts = [a + b for a, b in zip(parts[::2], parts[1::2])]
        return parts[0]

    def arrive(h, t, first):
        wait_for(recv_f.at[h, t - 1, pl.ds(0, 2 * COLS - 1)], rf_sem.at[h, t])
        if first:
            wait_linv(t)
            wait_for(rhs_sub_other.at[t - 1], lin_sem.at[5, t - 1])
        mine = rhs_sub[t, h] - add_up(recv_f.at[h, t - 1, pl.ds(r * COLS, COLS)], HALF)
        others = rhs_sub_other[t - 1, h] - add_up(recv_f.at[h, t - 1, pl.ds((1 - r) * COLS, COLS)], HALF)
        ylow[h, r] = dot_split(mine, linv_low[t - 1]).astype(BF16)
        ylow[h, 1 - r] = dot_split(others, linv_other[t - 1]).astype(BF16)
        return mine

    def finish(t, mine):
        for h, value in zip(streams, mine):
            keep(h, t)
            y_sub[t, h] = dot_full(value, linv[t])

    def level(t):
        mine = []
        for n, h in enumerate(streams):
            mine.append(arrive(h, t, n == 0))
            forward(h, t)
        finish(t, mine)

    pl.semaphore_wait(group_sem.at[3], 1)
    first.wait_recv()
    first.wait_send()
    for h in range(2):
        ylow[h, 1 - r] = ylow_swap[1, h]

    @pl.loop(0, COLS)
    def _(q):
        for h in range(2):
            pend[h, q] = jnp.zeros((HALF, WIDTH), F32)

    for h in streams:
        forward(h, 0, lambda k: lower_0[k])
    for h in streams:
        keep(h, 0)
    for i in (9, 5, 12, 13, 6, 7, 0, 1, 2, 3):
        copies[i].wait()
    sort_level(sub_src, sub_tgt, (1, 0), 1)
    mine = []
    for n, h in enumerate(streams):
        mine.append(arrive(h, 1, n == 0))
        forward(h, 1)
    finish(1, mine)
    for flip in (1, 2):
        pl.semaphore_signal(group_sem.at[flip - 1], inc=1, device_id=(l ^ flip, r, c), device_id_type=MESH)
    lin_copy(3)
    rhs_copy(3)
    sort_level(sub_src, sub_tgt, (2, 0), 2)

    @pl.loop(2, SUB - 1)
    def _(t):
        level(t)
        lin_copy(t + 2)

        @pl.when(t == 2)
        def _():
            rhs_copy(t + 2)

        @pl.when(t == 3)
        def _():
            rhs_top_copy(0)
            rhs_top_copy(1)

        sort_level(sub_src, sub_tgt, (t + 1, 0), t + 1)

    t = SUB - 1
    theirs = arrive(1 - half, t, True)
    products(1 - half, t, lambda k: lower[t, k])
    for q in range(COLS):
        core_out[0, q] = (share(1 - half, t, q) + pend[1 - half, q]).astype(BF16)
    core_copies = [to(other_core, core_out.at[0], core_in.at[0], misc_send.at[3], misc_recv.at[3])]
    mine = arrive(half, t, False)
    products(half, t, lambda k: lower[t, k])
    for q in range(COLS):
        halves[0, q] = share(half, t, q) + pend[half, q]
    core_copies[0].wait_recv()
    pl.semaphore_wait(group_sem.at[1], 1)
    slot_5 = high * 2 * COLS + me
    for i in ORDER:
        q = c ^ i
        send_ft[0, q] = (halves[0, q] + core_in[0, q].astype(F32)).astype(BF16)
        for flip in (2, 0):
            for j in (1, 0):
                if i or j or flip:
                    to((l ^ flip, r ^ j, q), send_ft.at[0, q], recv_5.at[slot_5], sf_sem.at[0, t], rf_sem.at[0, t + 1])
    recv_5[slot_5] = send_ft[0, c]
    for q in range(COLS):
        core_out[1, q] = share(1 - half, t, COLS + q).astype(BF16)
        halves[1, q] = share(half, t, COLS + q)
    core_copies.append(to(other_core, core_out.at[1], core_in.at[1], misc_send.at[4], misc_recv.at[4]))
    lin_copy(6)
    y_sub[t, 1 - half] = dot_full(theirs, linv[t])
    y_sub[t, half] = dot_full(mine, linv[t])
    core_copies[1].wait_recv()
    six[high] = (halves[1] + core_in[1].astype(F32)).astype(BF16)
    six_copy = to(other_high, six.at[high], six.at[high], misc_send.at[5], misc_recv.at[5])
    for t in (6, 5):
        uin_copy(t)
    sort_level(top_src, top_tgt, (0,), SUB)
    sort_level(top_src, top_tgt, (1,), SUB + 1)
    six_copy.wait_recv()
    for q in range(COLS):
        pend_top[q] = six[0, q].astype(F32) + six[1, q].astype(F32)

    def arrive_top(t, mine, others):
        mine = rhs_top[t] - mine
        if t < TOP - 1:
            wait_linv(t + SUB)
            wait_for(rhs_top_other.at[t], lin_sem.at[5, t + 4])
            ylow[0, r] = dot_split(mine, linv_low[t + SUB - 1]).astype(BF16)
            ylow[0, 1 - r] = dot_split(rhs_top_other[t] - others, linv_other[t + SUB - 1]).astype(BF16)
        return mine

    def forward_top(t):
        products(0, t + SUB, lambda k: lower[t + SUB, k])
        for i in ORDER:
            q = c ^ i
            value = share(0, t + SUB, q) + pend_top[q]
            send_ft[t + 1, q] = value.astype(BF16)
            for j in (1, 0):
                if i or j:
                    to((l, r ^ j, q), send_ft.at[t + 1, q], recv_ft.at[t, me], sf_sem.at[0, t + SUB], rf_sem.at[0, t + SUB + 1])
        recv_ft[t, me] = send_ft[t + 1, c]
        for u in (4 - 2 * t, 3 - 2 * t):
            uin_copy(u)
        if t == 0:
            for q in range(COLS):
                pend_top[q] = share(0, t + SUB, COLS + q)

    wait_for(recv_5.at[pl.ds(0, 4 * COLS - 1)], rf_sem.at[0, SUB])

    def add_up_5(row):
        return add_up(recv_5.at[pl.ds(row * COLS, COLS)], HALF) + add_up(
            recv_5.at[pl.ds((2 + row) * COLS, COLS)], HALF
        )

    value = arrive_top(0, add_up_5(r), add_up_5(1 - r))
    forward_top(0)
    y_top[0] = dot_full(value, linv[SUB])
    for t in (1, 2):
        wait_for(recv_ft.at[t - 1, pl.ds(0, 2 * COLS - 1)], rf_sem.at[0, t + SUB])
        mine = add_up(recv_ft.at[t - 1, pl.ds(r * COLS, COLS)], HALF)
        if t == 1:
            value = arrive_top(1, mine, add_up(recv_ft.at[t - 1, pl.ds((1 - r) * COLS, COLS)], HALF))
            forward_top(1)
            y_top[1] = dot_full(value, linv[SUB + 1])
            both_low[...] = dot_full(linv[7], uinv[7]).astype(BF16)
        else:
            value = arrive_top(2, mine, None)

    send_bt[2, 0] = dot_split(value, both_low[...]).astype(BF16)
    for i in ORDER:
        if i:
            to((l, r, c ^ i), send_bt.at[2, 0], recv_7.at[c], sb_sem.at[0, 7], rb_sem.at[0, 7])
    recv_7[c] = send_bt[2, 0]
    top_mine[2] = dot_full(dot_full(value, linv[7]), uinv[7])
    wait_for(recv_7.at[pl.ds(0, COLS - 1)], rb_sem.at[0, 7])
    x_top[pl.ds(COLS, COLS)] = recv_7[...]

    def down(t, load, src, row):
        total = None
        for k in range(SLOTS):
            value = dot(load(k), upper[t, k])
            taken = value * src[(*row, k)].astype(F32)
            total = value if total is None else total + value
            second = taken if k == 0 else second + taken
        at_first = r == 0
        parts = (total - second, second)
        return jnp.where(at_first, parts[0], parts[1]), jnp.where(at_first, parts[1], parts[0])

    def parts_of(t, mine, others, first=True):
        a = dot_split(mine, uinv_low[t - 1])
        if first:
            wait_for(uinv_other.at[t - 1], lin_sem.at[3, t - 1])
        b = -dot_split(others, uinv_other[t - 1])
        return a, b

    mine, others = down(6, lambda k: x_top[COLS + top_tgt[1, k] % COLS], top_src, (1,))
    mine = y_top[1] - mine
    a, b = parts_of(6, mine, others)
    send_bt[1, 0] = a.astype(BF16)
    send_bt[1, 1] = b.astype(BF16)
    for i in ORDER:
        to((l, 1 - r, c ^ i), send_bt.at[1, 1], recv_6.at[COLS + c], sb_sem.at[0, 6], rb_sem.at[0, 6])
        if i:
            to((l, r, c ^ i), send_bt.at[1, 0], recv_6.at[c], sb_sem.at[0, 6], rb_sem.at[0, 6])
    recv_6[c] = send_bt[1, 0]
    top_mine[1] = dot_full(mine, uinv[6])
    wait_for(recv_6.at[pl.ds(0, 2 * COLS - 1)], rb_sem.at[0, 6])
    for q in range(COLS):
        x_top[q] = (recv_6[q].astype(F32) + recv_6[COLS + q].astype(F32)).astype(BF16)
    top_mine[1] = top_mine[1] + recv_6[COLS + c].astype(F32)
    six_out[...] = x_top[pl.ds(0, COLS)]
    x6_copy = to(other_core, six_out, six_in, misc_send.at[7], misc_recv.at[7])

    mine, others = down(5, lambda k: x_top[top_tgt[0, k]], top_src, (0,))
    mine = y_top[0] - mine
    a, b = parts_of(5, mine, others)
    send_bt[0, 0] = a.astype(BF16)
    send_bt[0, 1] = b.astype(BF16)
    pl.semaphore_wait(group_sem.at[0], 1)
    slot_a = half * 2 * COLS + c
    for i in ORDER:
        for flip in (1, 0):
            to((l ^ flip, 1 - r, c ^ i), send_bt.at[0, 1], recv_b5.at[slot_a + COLS], sb_sem.at[0, 5], rb_sem.at[0, 5])
            if i or flip:
                to((l ^ flip, r, c ^ i), send_bt.at[0, 0], recv_b5.at[slot_a], sb_sem.at[0, 5], rb_sem.at[0, 5])
    recv_b5[slot_a] = send_bt[0, 0]
    top_mine[0] = dot_full(mine, uinv[5])
    x6_copy.wait_recv()
    for q in range(COLS):
        x_sub[half, 6 * COLS + q] = x_top[q]
        x_sub[1 - half, 6 * COLS + q] = six_in[q]
    wait_for(recv_b5.at[pl.ds(0, 4 * COLS - 1)], rb_sem.at[0, 5])
    for q in range(COLS):
        for h in range(2):
            x_sub[h, 5 * COLS + q] = (
                recv_b5[h * 2 * COLS + q].astype(F32) + recv_b5[h * 2 * COLS + COLS + q].astype(F32)
            ).astype(BF16)
    top_mine[0] = top_mine[0] + recv_b5[slot_a + COLS].astype(F32)
    top_copy = to(other_core, top_mine, top_other, misc_send.at[6], misc_recv.at[6])

    def down_sub(h, t):
        return down(t, lambda k: x_sub[h, (t + 1) * COLS + sub_tgt[t, 0, k]], sub_src, (t, 0))

    def climb_down(h, t):
        mine, others = down_sub(h, t)
        mine = y_sub[t, h] - mine
        a, b = parts_of(t, mine, others, h is streams[0])
        send_b[h, t, 0] = a.astype(BF16)
        send_b[h, t, 1] = b.astype(BF16)
        for i in ORDER:
            to((l, 1 - r, c ^ i), send_b.at[h, t, 1], recv_b.at[h, t, COLS + c], sb_sem.at[h, t], rb_sem.at[h, t])
            if i:
                to((l, r, c ^ i), send_b.at[h, t, 0], recv_b.at[h, t, c], sb_sem.at[h, t], rb_sem.at[h, t])
        recv_b[h, t, c] = send_b[h, t, 0]
        return mine

    def solved(h, t):
        wait_for(recv_b.at[h, t, pl.ds(0, 2 * COLS - 1)], rb_sem.at[h, t])
        for q in range(COLS):
            x_sub[h, t * COLS + q] = (recv_b[h, t, q].astype(F32) + recv_b[h, t, COLS + q].astype(F32)).astype(BF16)

    def put_out(h, t, mine):
        rows = pl.ds(pl.multiple_of(h * HALF, HALF), HALF)
        sub_out[t, rows] = dot_full(mine, uinv[t]) + recv_b[h, t, COLS + c].astype(F32)

    kept = [climb_down(h, SUB - 1) for h in streams]

    def descend(step, kept):
        t = SUB - 2 - step
        later = []
        for h in streams:
            solved(h, t + 1)
            later.append(climb_down(h, t))
        for h, value in zip(streams, kept):
            put_out(h, t + 1, value)
        return tuple(later)

    kept = lax.fori_loop(0, SUB - 2, descend, tuple(kept))
    mine, last = [], []
    for n, h in enumerate(streams):
        solved(h, 1)
        value, others = down_sub(h, 0)
        mine.append(value)
        last_out[h] = others
        last.append(to(other_row, last_out.at[h], last_in.at[h], misc_send.at[8 + n], misc_recv.at[8 + n]))
    for h, value in zip(streams, kept):
        put_out(h, 1, value)
    top_copy.wait_recv()
    for t in range(TOP):
        top_out[t, half_rows] = top_mine[t]
        top_out[t, pl.ds(pl.multiple_of((1 - half) * HALF, HALF), HALF)] = top_other[t]

    for copy in (*core_copies, six_copy, x6_copy, top_copy):
        copy.wait_send()
    for t in range(6):
        wait_for(linv_other.at[t], lin_sem.at[0, t])
        wait_for(uinv_other.at[t], lin_sem.at[2, t])
        wait_for(rhs_sub_other.at[t] if t < 4 else rhs_top_other.at[t - 4], lin_sem.at[4, t])
    for t in range(SUB - 1):
        for h in range(2):
            wait_for(recv_f.at[h, t, pl.ds(0, 2 * COLS - 1)], sf_sem.at[h, t])
    wait_for(recv_5.at[pl.ds(0, 4 * COLS - 1)], sf_sem.at[0, 4])
    wait_for(recv_ft.at[0, pl.ds(0, 2 * COLS - 1)], sf_sem.at[0, 5])
    wait_for(recv_ft.at[1, pl.ds(0, 2 * COLS - 1)], sf_sem.at[0, 6])
    wait_for(recv_7.at[pl.ds(0, COLS - 1)], sb_sem.at[0, 7])
    wait_for(recv_6.at[pl.ds(0, 2 * COLS - 1)], sb_sem.at[0, 6])
    wait_for(recv_b5.at[pl.ds(0, 4 * COLS - 1)], sb_sem.at[0, 5])
    for t in range(1, SUB):
        for h in range(2):
            wait_for(recv_b.at[h, t, pl.ds(0, 2 * COLS - 1)], sb_sem.at[h, t])
    for h, value, copy in zip(streams, mine, last):
        copy.wait_send()
        copy.wait_recv()
        rows = pl.ds(pl.multiple_of(h * HALF, HALF), HALF)
        sub_out[0, rows] = dot_full(y_sub[0, h] - value - last_in[h], uinv[0])


def hand_over(sub, top):
    def body(sub_in, top_in, sub_res, top_res):
        sub_res[0, 0, 0] = sub_in[...]
        top_res[0, 0] = top_in[...]

    vmem_spec = pl.BlockSpec(memory_space=pltpu.VMEM)
    return pl.pallas_call(
        body,
        out_shape=(
            jax.ShapeDtypeStruct((1, 1, 1) + sub.shape, F32),
            jax.ShapeDtypeStruct((1, 1) + top.shape, F32),
        ),
        in_specs=[vmem_spec] * 2,
        out_specs=[vmem_spec] * 2,
    )(sub, top)


def local(*args):
    flat = [a.reshape(a.shape[3:] if i < 7 else a.shape[2:]) for i, a in enumerate(args)]
    flat[0] = args[0].reshape(SUB, 2, HALF, WIDTH)
    flat[5], flat[6] = (a.reshape(SUB, 1, SLOTS) for a in args[5:7])
    vmem, smem, dma = pltpu.VMEM, pltpu.SMEM, pltpu.SemaphoreType.DMA
    tile = (SIDES, WIDTH)
    half = (HALF, WIDTH)
    block = (WIDTH, WIDTH)
    scratch = [
        smem((SUB, 1, SLOTS), jnp.int32),
        smem((SUB, 1, SLOTS), jnp.int32),
        smem((TOP - 1, SLOTS), jnp.int32),
        smem((TOP - 1, SLOTS), jnp.int32),
        vmem((SLOTS,) + block, BF16),
        vmem((LINKED, SLOTS) + block, BF16),
        vmem((LINKED, SLOTS) + block, BF16),
        vmem((SUB + TOP,) + block, F32),
        vmem((SUB + TOP,) + block, F32),
        vmem((SUB, 2) + half, F32),
        vmem((TOP,) + half, F32),
        vmem((6,) + block, BF16),
        vmem((6,) + block, BF16),
        vmem((6,) + block, BF16),
        vmem((6,) + block, BF16),
        vmem((SUB - 1, 2) + half, F32),
        vmem((2,) + half, F32),
        smem((LINKED, SLOTS), jnp.int32),
        smem((LINKED, SLOTS), jnp.int32),
        smem((LINKED, 2 * COLS + 1), jnp.int32),
        vmem((2, 2) + half, BF16),
        vmem((2, 2) + half, BF16),
        vmem((SUB, 2) + half, F32),
        vmem((TOP,) + half, F32),
        vmem((2, SLOTS + 1) + half, F32),
        vmem((2, COLS) + half, F32),
        vmem((COLS,) + half, F32),
        vmem((2, SUB - 1, COLS) + half, BF16),
        vmem((2, SUB - 1, 2 * COLS) + half, BF16),
        vmem((TOP, COLS) + half, BF16),
        vmem((4 * COLS,) + half, BF16),
        vmem((2, 2 * COLS) + half, BF16),
        vmem((2, COLS) + half, F32),
        vmem((2, COLS) + half, BF16),
        vmem((2, COLS) + half, BF16),
        vmem((2, COLS) + half, BF16),
        vmem((2, 7 * COLS) + half, BF16),
        vmem((2 * COLS,) + half, BF16),
        vmem((2, SUB, 2) + half, BF16),
        vmem((2, SUB, 2 * COLS) + half, BF16),
        vmem((TOP, 2) + half, BF16),
        vmem((COLS,) + half, BF16),
        vmem((2 * COLS,) + half, BF16),
        vmem((4 * COLS,) + half, BF16),
        vmem((COLS,) + half, BF16),
        vmem((COLS,) + half, BF16),
        vmem((2,) + half, F32),
        vmem((2,) + half, F32),
        vmem((TOP,) + half, F32),
        vmem((TOP,) + half, F32),
        vmem(block, BF16),
        dma((15,)),
        dma((6, 6)),
        pltpu.SemaphoreType.REGULAR((4,)),
        dma((10,)),
        dma((10,)),
        dma((2, SUB + TOP)),
        dma((2, SUB + TOP)),
        dma((2, SUB + TOP)),
        dma((2, SUB + TOP)),
    ]
    any_spec = pl.BlockSpec(memory_space=pl.ANY)
    vmem_spec = pl.BlockSpec(memory_space=pltpu.VMEM)
    sub, top = pl.pallas_call(
        kernel,
        out_shape=(
            jax.ShapeDtypeStruct((SUB,) + tile, F32),
            jax.ShapeDtypeStruct((TOP,) + tile, F32),
        ),
        in_specs=[any_spec] * 14,
        out_specs=(vmem_spec, vmem_spec),
        scratch_shapes=scratch,
        compiler_params=pltpu.CompilerParams(
            collective_id=0, has_side_effects=True, vmem_limit_bytes=60 * 1024 * 1024
        ),
    )(*flat)
    return hand_over(sub, top)


def solution(mesh):
    sub = P("layer", "prow", "pcol")
    top = P("prow", "pcol")
    return jax.shard_map(
        local, mesh=mesh, in_specs=(sub,) * 7 + (top,) * 7, out_specs=(sub, top), check_vma=False
    )
```

```python
import jax
import jax.numpy as jnp
from jax import lax
from jax.experimental import pallas as pl
from jax.experimental.pallas import tpu as pltpu
from jax.sharding import PartitionSpec as P

MESH = pl.DeviceIdType.MESH
F32 = jnp.float32
BF16 = jnp.bfloat16
SUB, TOP, SLOTS, COLS, SIDES, WIDTH = 5, 3, 16, 16, 32, 128
HALF = SIDES // 2
LINKED = SUB + TOP - 1
ORDER = (10, 9, 11, 6, 14, 5, 7, 13, 15, 8, 2, 1, 3, 4, 12, 0)


def dot(a, b):
    return jnp.dot(a, b, preferred_element_type=F32)


def dot_full(a, b):
    return jnp.dot(a, b, preferred_element_type=F32, precision=lax.Precision.HIGHEST)


def dot_split(a, b):
    high = a.astype(BF16)
    low = (a - high.astype(F32)).astype(BF16)
    return dot(high, b) + dot(low, b)


def wait_for(ref, sem):
    pltpu.make_async_copy(ref, ref, sem).wait()


def kernel(
    sub_rhs, sub_linv, sub_uinv, sub_lower, sub_upper, sub_src_in, sub_tgt_in,
    top_rhs, top_linv, top_uinv, top_lower, top_upper, top_src_in, top_tgt_in,
    sub_out, top_out,
    sub_src, sub_tgt, top_src, top_tgt,
    lower_0, lower, upper, linv, uinv, rhs_sub, rhs_top,
    linv_low, uinv_low, linv_other, uinv_other, pair, rhs_sub_other, rhs_top_other,
    perm, psrc, ends,
    ylow, ylow_swap, yu_sub, yu_top, sums, pend, pend_top,
    send_f, recv_f, send_ft, recv_5, recv_ft,
    halves, core_out, core_in, six,
    x_sub, x_top, send_b, recv_b, send_bt, recv_7, recv_6, recv_b5, six_in, six_out, last_out, last_in, top_mine, top_other,
    both_low, load_sem, lin_sem, group_sem, misc_recv, misc_send, rf_sem, sf_sem, rb_sem, sb_sem,
):
    l, r, c = lax.axis_index("layer"), lax.axis_index("prow"), lax.axis_index("pcol")
    high, half = l // 2, l % 2
    half_rows = pl.ds(pl.multiple_of(half * HALF, HALF), HALF)
    me = r * COLS + c

    loads = (
        (sub_lower.at[pl.ds(1, SUB - 1)], lower.at[pl.ds(1, SUB - 1)]),
        (top_lower, lower.at[pl.ds(SUB, TOP - 1)]),
        (sub_upper, upper.at[pl.ds(0, SUB)]),
        (top_upper, upper.at[pl.ds(SUB, TOP - 1)]),
        (sub_linv, linv.at[pl.ds(0, SUB)]),
        (top_linv, linv.at[pl.ds(SUB, TOP)]),
        (sub_uinv, uinv.at[pl.ds(0, SUB)]),
        (top_uinv, uinv.at[pl.ds(SUB, TOP)]),
        (sub_rhs, rhs_sub),
        (top_rhs.at[:, half_rows], rhs_top),
        (sub_src_in, sub_src),
        (sub_tgt_in, sub_tgt),
        (top_src_in, top_src),
        (top_tgt_in, top_tgt),
        (sub_lower.at[0], lower_0),
    )
    copies = [pltpu.make_async_copy(a, b, load_sem.at[i]) for i, (a, b) in enumerate(loads)]
    for i in (8, 4, 10, 11, 14, 9, 5, 12, 13, 0, 1):
        copies[i].start()

    barrier = pltpu.get_barrier_semaphore()
    for flip in (1, 2):
        pl.semaphore_signal(barrier, inc=1, device_id=(l ^ flip, r, c), device_id_type=MESH)
    pl.semaphore_signal(barrier, inc=1, device_id=(l, 1 - r, c), device_id_type=MESH)
    for i in (1, 2, 3, 4, 8, 12):
        pl.semaphore_signal(barrier, inc=1, device_id=(l, r, c ^ i), device_id_type=MESH)

    def sort_level(src, tgt, row, t):
        codes = [tgt[(*row, k)] for k in range(SLOTS)]
        rank = [jnp.int32(0)] * SLOTS
        for k in range(SLOTS):
            for j in range(k):
                before = (codes[j] <= codes[k]).astype(jnp.int32)
                rank[k] = rank[k] + before
                rank[j] = rank[j] + (1 - before)
        for i in range(SLOTS):
            slot = jnp.int32(0)
            for k in range(1, SLOTS):
                slot = slot + jnp.where(rank[k] == i, k, 0)
            perm[t, i] = slot
            psrc[t, i] = src[(*row, slot)]
        ends[t, 0] = 0
        for q in range(2 * COLS):
            count = jnp.int32(0)
            for k in range(SLOTS):
                count = count + (codes[k] <= q).astype(jnp.int32)
            ends[t, q + 1] = count

    copies[8].wait()
    copies[4].wait()
    y0 = dot_full(rhs_sub[0].reshape(SIDES, WIDTH), linv[0]).reshape(2, HALF, WIDTH)
    ylow_swap[0] = y0.astype(BF16)
    for h in range(2):
        ylow[h, r] = ylow_swap[0, h]
    pl.semaphore_wait(barrier, 9)

    def to(device, src, dst, send_sem, recv_sem):
        copy = pltpu.make_async_remote_copy(
            src_ref=src, dst_ref=dst, send_sem=send_sem, recv_sem=recv_sem, device_id=device, device_id_type=MESH
        )
        copy.start()
        return copy

    other_row = (l, 1 - r, c)
    other_core = (l ^ 1, r, c)
    other_high = (l ^ 2, r, c)

    first = to(other_row, ylow_swap.at[0], ylow_swap.at[1], misc_send.at[0], misc_recv.at[0])
    for i in (4, 8, 12):
        pl.semaphore_signal(group_sem.at[2], inc=1, device_id=(l, r, c ^ i), device_id_type=MESH)
    copies[10].wait()
    copies[11].wait()
    sort_level(sub_src, sub_tgt, (0, 0), 0)

    def lin_copy(t):
        linv_low[t - 1] = linv[t].astype(BF16)
        return to(other_row, linv_low.at[t - 1], linv_other.at[t - 1], lin_sem.at[0, t - 1], lin_sem.at[1, t - 1])

    def uin_copy(t):
        uinv_low[t] = uinv[t].astype(BF16)
        return to(other_row, uinv_low.at[t], uinv_other.at[t], lin_sem.at[2, t], lin_sem.at[3, t])

    def rhs_copy(t):
        return to(other_row, rhs_sub.at[t], rhs_sub_other.at[t - 1], lin_sem.at[4, t - 1], lin_sem.at[5, t - 1])

    def rhs_top_copy(t):
        return to(other_row, rhs_top.at[t], rhs_top_other.at[t], lin_sem.at[4, t + 4], lin_sem.at[5, t + 4])

    pl.semaphore_wait(group_sem.at[2], 3)
    pl.semaphore_signal(group_sem.at[3], inc=1, device_id=other_row, device_id_type=MESH)
    lin_copy(1)
    rhs_copy(1)
    copies[14].wait()

    def prepare_lower(t, src, row):
        wait_for(linv_other.at[t - 1], lin_sem.at[1, t - 1])
        pair[r] = linv_low[t - 1]
        pair[1 - r] = linv_other[t - 1]
        for k in range(SLOTS):
            lower[t, k] = dot(pair[src[(*row, k)]], lower[t, k]).astype(BF16)

    def prepare_upper(t, src, row):
        wait_for(uinv_other.at[t], lin_sem.at[3, t])
        pair[r] = uinv_low[t]
        pair[1 - r] = uinv_other[t]
        for k in range(SLOTS):
            upper[t, k] = dot(upper[t, k], pair[src[(*row, k)]]).astype(BF16)

    def solve_both(value, t):
        return dot_full(dot_full(value, linv[t]), uinv[t])

    streams = (1 - half, half)

    def products(h, t, block):
        total = jnp.zeros((HALF, WIDTH), F32)
        sums[h, 0] = total
        for i in range(SLOTS):
            total = total + dot(ylow[h, psrc[t, i]], block(perm[t, i]))
            sums[h, i + 1] = total

    def share(h, t, code):
        return sums[h, ends[t, code + 1]] - sums[h, ends[t, code]]

    def forward(h, t, block=None):
        products(h, t, block or (lambda k: lower[t, k]))
        for i in ORDER:
            q = c ^ i
            send_f[h, t, q] = (share(h, t, q) + pend[h, q]).astype(BF16)
            for j in (1, 0):
                if i or j:
                    to((l, r ^ j, q), send_f.at[h, t, q], recv_f.at[h, t, me], sf_sem.at[h, t], rf_sem.at[h, t + 1])
        recv_f[h, t, me] = send_f[h, t, c]

    def keep(h, t):
        for q in range(COLS):
            pend[h, q] = share(h, t, COLS + q)

    def add_up(ref, rows):
        parts = [ref[i].astype(F32) for i in range(COLS)]
        while len(parts) > 1:
            parts = [a + b for a, b in zip(parts[::2], parts[1::2])]
        return parts[0]

    def arrive(h, t, first):
        wait_for(recv_f.at[h, t - 1, pl.ds(0, 2 * COLS - 1)], rf_sem.at[h, t])
        if first:
            wait_for(rhs_sub_other.at[t - 1], lin_sem.at[5, t - 1])
        mine = rhs_sub[t, h] - add_up(recv_f.at[h, t - 1, pl.ds(r * COLS, COLS)], HALF)
        others = rhs_sub_other[t - 1, h] - add_up(recv_f.at[h, t - 1, pl.ds((1 - r) * COLS, COLS)], HALF)
        ylow[h, r] = mine.astype(BF16)
        ylow[h, 1 - r] = others.astype(BF16)
        return mine

    def finish(t, mine):
        for h, value in zip(streams, mine):
            keep(h, t)
            yu_sub[t, h] = solve_both(value, t)

    def level(t):
        mine = []
        for n, h in enumerate(streams):
            mine.append(arrive(h, t, n == 0))
            forward(h, t)
        finish(t, mine)

    pl.semaphore_wait(group_sem.at[3], 1)
    first.wait_recv()
    first.wait_send()
    for h in range(2):
        ylow[h, 1 - r] = ylow_swap[1, h]

    @pl.loop(0, COLS)
    def _(q):
        for h in range(2):
            pend[h, q] = jnp.zeros((HALF, WIDTH), F32)

    for h in streams:
        forward(h, 0, lambda k: lower_0[k])
    for i in (6, 7, 2, 3):
        copies[i].start()
    for h in streams:
        keep(h, 0)
    for i in (9, 5, 12, 13, 0, 1):
        copies[i].wait()
    lin_copy(2)
    rhs_copy(2)
    sort_level(sub_src, sub_tgt, (1, 0), 1)
    prepare_lower(1, sub_src, (1, 0))
    for i in (6, 7, 2, 3):
        copies[i].wait()
    yu_sub[0] = dot_full(y0.reshape(SIDES, WIDTH), uinv[0]).reshape(2, HALF, WIDTH)
    mine = []
    for n, h in enumerate(streams):
        mine.append(arrive(h, 1, n == 0))
        forward(h, 1)
    finish(1, mine)
    for flip in (1, 2):
        pl.semaphore_signal(group_sem.at[flip - 1], inc=1, device_id=(l ^ flip, r, c), device_id_type=MESH)
    lin_copy(3)
    rhs_copy(3)
    sort_level(sub_src, sub_tgt, (2, 0), 2)
    prepare_lower(2, sub_src, (2, 0))

    @pl.loop(2, SUB - 1)
    def _(t):
        level(t)
        lin_copy(t + 2)

        @pl.when(t == 2)
        def _():
            rhs_copy(t + 2)

        @pl.when(t == 3)
        def _():
            rhs_top_copy(0)
            rhs_top_copy(1)

        sort_level(sub_src, sub_tgt, (t + 1, 0), t + 1)
        prepare_lower(t + 1, sub_src, (t + 1, 0))

    t = SUB - 1
    theirs = arrive(1 - half, t, True)
    products(1 - half, t, lambda k: lower[t, k])
    for q in range(COLS):
        core_out[0, q] = (share(1 - half, t, q) + pend[1 - half, q]).astype(BF16)
    core_copies = [to(other_core, core_out.at[0], core_in.at[0], misc_send.at[3], misc_recv.at[3])]
    mine = arrive(half, t, False)
    products(half, t, lambda k: lower[t, k])
    for q in range(COLS):
        halves[0, q] = share(half, t, q) + pend[half, q]
    core_copies[0].wait_recv()
    pl.semaphore_wait(group_sem.at[1], 1)
    slot_5 = high * 2 * COLS + me
    for i in ORDER:
        q = c ^ i
        send_ft[0, q] = (halves[0, q] + core_in[0, q].astype(F32)).astype(BF16)
        for flip in (2, 0):
            for j in (1, 0):
                if i or j or flip:
                    to((l ^ flip, r ^ j, q), send_ft.at[0, q], recv_5.at[slot_5], sf_sem.at[0, t], rf_sem.at[0, t + 1])
    recv_5[slot_5] = send_ft[0, c]
    for q in range(COLS):
        core_out[1, q] = share(1 - half, t, COLS + q).astype(BF16)
        halves[1, q] = share(half, t, COLS + q)
    core_copies.append(to(other_core, core_out.at[1], core_in.at[1], misc_send.at[4], misc_recv.at[4]))
    lin_copy(6)
    yu_sub[t, 1 - half] = solve_both(theirs, t)
    yu_sub[t, half] = solve_both(mine, t)
    core_copies[1].wait_recv()
    six[high] = (halves[1] + core_in[1].astype(F32)).astype(BF16)
    six_copy = to(other_high, six.at[high], six.at[high], misc_send.at[5], misc_recv.at[5])
    sort_level(top_src, top_tgt, (0,), SUB)
    sort_level(top_src, top_tgt, (1,), SUB + 1)
    prepare_lower(SUB, top_src, (0,))
    six_copy.wait_recv()
    for q in range(COLS):
        pend_top[q] = six[0, q].astype(F32) + six[1, q].astype(F32)

    def arrive_top(t, mine, others):
        mine = rhs_top[t] - mine
        if t < TOP - 1:
            wait_for(rhs_top_other.at[t], lin_sem.at[5, t + 4])
            ylow[0, r] = mine.astype(BF16)
            ylow[0, 1 - r] = (rhs_top_other[t] - others).astype(BF16)
        return mine

    def forward_top(t):
        products(0, t + SUB, lambda k: lower[t + SUB, k])
        for i in ORDER:
            q = c ^ i
            value = share(0, t + SUB, q) + pend_top[q]
            send_ft[t + 1, q] = value.astype(BF16)
            for j in (1, 0) if t == 0 else (0,):
                if i or j:
                    to((l, r ^ j, q), send_ft.at[t + 1, q], recv_ft.at[t, me if t == 0 else c], sf_sem.at[0, t + SUB], rf_sem.at[0, t + SUB + 1])
        recv_ft[t, me if t == 0 else c] = send_ft[t + 1, c]
        if t == 0:
            for q in range(COLS):
                pend_top[q] = share(0, t + SUB, COLS + q)
            uin_copy(6)
        else:
            for u in (5, 4, 3):
                uin_copy(u)

    wait_for(recv_5.at[pl.ds(0, 4 * COLS - 1)], rf_sem.at[0, SUB])

    def add_up_5(row):
        return add_up(recv_5.at[pl.ds(row * COLS, COLS)], HALF) + add_up(
            recv_5.at[pl.ds((2 + row) * COLS, COLS)], HALF
        )

    value = arrive_top(0, add_up_5(r), add_up_5(1 - r))
    forward_top(0)
    prepare_lower(SUB + 1, top_src, (1,))
    yu_top[0] = solve_both(value, SUB)
    for t in (1, 2):
        wait_for(recv_ft.at[t - 1, pl.ds(0, (2 * COLS if t == 1 else COLS) - 1)], rf_sem.at[0, t + SUB])
        mine = add_up(recv_ft.at[t - 1, pl.ds(r * COLS if t == 1 else 0, COLS)], HALF)
        if t == 1:
            value = arrive_top(1, mine, add_up(recv_ft.at[t - 1, pl.ds((1 - r) * COLS, COLS)], HALF))
            forward_top(1)
            yu_top[1] = solve_both(value, SUB + 1)
            both_low[...] = dot_full(linv[7], uinv[7]).astype(BF16)
        else:
            value = arrive_top(2, mine, None)

    send_bt[2, 0] = dot_split(value, both_low[...]).astype(BF16)
    for i in ORDER:
        if i:
            to((l, r, c ^ i), send_bt.at[2, 0], recv_7.at[c], sb_sem.at[0, 7], rb_sem.at[0, 7])
    recv_7[c] = send_bt[2, 0]
    top_mine[2] = dot_full(dot_full(value, linv[7]), uinv[7])
    for u in (2, 1, 0):
        uin_copy(u)
    prepare_upper(6, top_src, (1,))
    wait_for(recv_7.at[pl.ds(0, COLS - 1)], rb_sem.at[0, 7])
    x_top[pl.ds(COLS, COLS)] = recv_7[...]

    def down(t, load, src, row):
        total = None
        for k in range(SLOTS):
            value = dot(load(k), upper[t, k])
            taken = value * src[(*row, k)].astype(F32)
            total = value if total is None else total + value
            second = taken if k == 0 else second + taken
        at_first = r == 0
        parts = (total - second, second)
        return jnp.where(at_first, parts[0], parts[1]), jnp.where(at_first, parts[1], parts[0])

    mine, others = down(6, lambda k: x_top[COLS + top_tgt[1, k] % COLS], top_src, (1,))
    a, b = yu_top[1] - mine, -others
    send_bt[1, 0] = a.astype(BF16)
    send_bt[1, 1] = b.astype(BF16)
    for i in ORDER:
        to((l, 1 - r, c ^ i), send_bt.at[1, 1], recv_6.at[COLS + c], sb_sem.at[0, 6], rb_sem.at[0, 6])
        if i:
            to((l, r, c ^ i), send_bt.at[1, 0], recv_6.at[c], sb_sem.at[0, 6], rb_sem.at[0, 6])
    recv_6[c] = send_bt[1, 0]
    top_mine[1] = a
    prepare_upper(5, top_src, (0,))
    wait_for(recv_6.at[pl.ds(0, 2 * COLS - 1)], rb_sem.at[0, 6])
    for q in range(COLS):
        x_top[q] = (recv_6[q].astype(F32) + recv_6[COLS + q].astype(F32)).astype(BF16)
    top_mine[1] = top_mine[1] + recv_6[COLS + c].astype(F32)
    six_out[...] = x_top[pl.ds(0, COLS)]
    x6_copy = to(other_core, six_out, six_in, misc_send.at[7], misc_recv.at[7])

    mine, others = down(5, lambda k: x_top[top_tgt[0, k]], top_src, (0,))
    a, b = yu_top[0] - mine, -others
    send_bt[0, 0] = a.astype(BF16)
    send_bt[0, 1] = b.astype(BF16)
    pl.semaphore_wait(group_sem.at[0], 1)
    slot_a = half * 2 * COLS + c
    for i in ORDER:
        for flip in (1, 0):
            to((l ^ flip, 1 - r, c ^ i), send_bt.at[0, 1], recv_b5.at[slot_a + COLS], sb_sem.at[0, 5], rb_sem.at[0, 5])
            if i or flip:
                to((l ^ flip, r, c ^ i), send_bt.at[0, 0], recv_b5.at[slot_a], sb_sem.at[0, 5], rb_sem.at[0, 5])
    recv_b5[slot_a] = send_bt[0, 0]
    top_mine[0] = a
    prepare_upper(4, sub_src, (4, 0))
    x6_copy.wait_recv()
    for q in range(COLS):
        x_sub[half, 6 * COLS + q] = x_top[q]
        x_sub[1 - half, 6 * COLS + q] = six_in[q]
    wait_for(recv_b5.at[pl.ds(0, 4 * COLS - 1)], rb_sem.at[0, 5])
    for q in range(COLS):
        for h in range(2):
            x_sub[h, 5 * COLS + q] = (
                recv_b5[h * 2 * COLS + q].astype(F32) + recv_b5[h * 2 * COLS + COLS + q].astype(F32)
            ).astype(BF16)
    top_mine[0] = top_mine[0] + recv_b5[slot_a + COLS].astype(F32)
    top_copy = to(other_core, top_mine, top_other, misc_send.at[6], misc_recv.at[6])

    def down_sub(h, t):
        return down(t, lambda k: x_sub[h, (t + 1) * COLS + sub_tgt[t, 0, k]], sub_src, (t, 0))

    def climb_down(h, t):
        mine, others = down_sub(h, t)
        a, b = yu_sub[t, h] - mine, -others
        send_b[h, t, 0] = a.astype(BF16)
        send_b[h, t, 1] = b.astype(BF16)
        for i in ORDER:
            to((l, 1 - r, c ^ i), send_b.at[h, t, 1], recv_b.at[h, t, COLS + c], sb_sem.at[h, t], rb_sem.at[h, t])
            if i:
                to((l, r, c ^ i), send_b.at[h, t, 0], recv_b.at[h, t, c], sb_sem.at[h, t], rb_sem.at[h, t])
        recv_b[h, t, c] = send_b[h, t, 0]
        return a

    def solved(h, t):
        wait_for(recv_b.at[h, t, pl.ds(0, 2 * COLS - 1)], rb_sem.at[h, t])
        for q in range(COLS):
            x_sub[h, t * COLS + q] = (recv_b[h, t, q].astype(F32) + recv_b[h, t, COLS + q].astype(F32)).astype(BF16)

    def put_out(h, t, mine):
        rows = pl.ds(pl.multiple_of(h * HALF, HALF), HALF)
        sub_out[t, rows] = mine + recv_b[h, t, COLS + c].astype(F32)

    kept = [climb_down(h, SUB - 1) for h in streams]
    prepare_upper(SUB - 2, sub_src, (SUB - 2, 0))

    def descend(step, kept):
        t = SUB - 2 - step
        later = []
        for h in streams:
            solved(h, t + 1)
            later.append(climb_down(h, t))
        for h, value in zip(streams, kept):
            put_out(h, t + 1, value)
        prepare_upper(t - 1, sub_src, (t - 1, 0))
        return tuple(later)

    kept = lax.fori_loop(0, SUB - 2, descend, tuple(kept))
    mine, last = [], []
    for n, h in enumerate(streams):
        solved(h, 1)
        value, others = down_sub(h, 0)
        mine.append(yu_sub[0, h] - value)
        last_out[h] = -others
        last.append(to(other_row, last_out.at[h], last_in.at[h], misc_send.at[8 + n], misc_recv.at[8 + n]))
    for h, value in zip(streams, kept):
        put_out(h, 1, value)
    top_copy.wait_recv()
    for t in range(TOP):
        top_out[t, half_rows] = top_mine[t]
        top_out[t, pl.ds(pl.multiple_of((1 - half) * HALF, HALF), HALF)] = top_other[t]

    for copy in (*core_copies, six_copy, x6_copy, top_copy):
        copy.wait_send()
    for t in range(LINKED):
        wait_for(uinv_other.at[t], lin_sem.at[2, t])
    for t in range(6):
        wait_for(linv_other.at[t], lin_sem.at[0, t])
        wait_for(rhs_sub_other.at[t] if t < 4 else rhs_top_other.at[t - 4], lin_sem.at[4, t])
    for t in range(SUB - 1):
        for h in range(2):
            wait_for(recv_f.at[h, t, pl.ds(0, 2 * COLS - 1)], sf_sem.at[h, t])
    wait_for(recv_5.at[pl.ds(0, 4 * COLS - 1)], sf_sem.at[0, 4])
    wait_for(recv_ft.at[0, pl.ds(0, 2 * COLS - 1)], sf_sem.at[0, 5])
    wait_for(recv_ft.at[1, pl.ds(0, COLS - 1)], sf_sem.at[0, 6])
    wait_for(recv_7.at[pl.ds(0, COLS - 1)], sb_sem.at[0, 7])
    wait_for(recv_6.at[pl.ds(0, 2 * COLS - 1)], sb_sem.at[0, 6])
    wait_for(recv_b5.at[pl.ds(0, 4 * COLS - 1)], sb_sem.at[0, 5])
    for t in range(1, SUB):
        for h in range(2):
            wait_for(recv_b.at[h, t, pl.ds(0, 2 * COLS - 1)], sb_sem.at[h, t])
    for h, value, copy in zip(streams, mine, last):
        copy.wait_send()
        copy.wait_recv()
        rows = pl.ds(pl.multiple_of(h * HALF, HALF), HALF)
        sub_out[0, rows] = value + last_in[h]


def hand_over(sub, top):
    def body(sub_in, top_in, sub_res, top_res):
        sub_res[0, 0, 0] = sub_in[...]
        top_res[0, 0] = top_in[...]

    vmem_spec = pl.BlockSpec(memory_space=pltpu.VMEM)
    return pl.pallas_call(
        body,
        out_shape=(
            jax.ShapeDtypeStruct((1, 1, 1) + sub.shape, F32),
            jax.ShapeDtypeStruct((1, 1) + top.shape, F32),
        ),
        in_specs=[vmem_spec] * 2,
        out_specs=[vmem_spec] * 2,
    )(sub, top)


def local(*args):
    flat = [a.reshape(a.shape[3:] if i < 7 else a.shape[2:]) for i, a in enumerate(args)]
    flat[0] = args[0].reshape(SUB, 2, HALF, WIDTH)
    flat[5], flat[6] = (a.reshape(SUB, 1, SLOTS) for a in args[5:7])
    vmem, smem, dma = pltpu.VMEM, pltpu.SMEM, pltpu.SemaphoreType.DMA
    tile = (SIDES, WIDTH)
    half = (HALF, WIDTH)
    block = (WIDTH, WIDTH)
    scratch = [
        smem((SUB, 1, SLOTS), jnp.int32),
        smem((SUB, 1, SLOTS), jnp.int32),
        smem((TOP - 1, SLOTS), jnp.int32),
        smem((TOP - 1, SLOTS), jnp.int32),
        vmem((SLOTS,) + block, BF16),
        vmem((LINKED, SLOTS) + block, BF16),
        vmem((LINKED, SLOTS) + block, BF16),
        vmem((SUB + TOP,) + block, F32),
        vmem((SUB + TOP,) + block, F32),
        vmem((SUB, 2) + half, F32),
        vmem((TOP,) + half, F32),
        vmem((6,) + block, BF16),
        vmem((LINKED,) + block, BF16),
        vmem((6,) + block, BF16),
        vmem((LINKED,) + block, BF16),
        vmem((2,) + block, BF16),
        vmem((SUB - 1, 2) + half, F32),
        vmem((2,) + half, F32),
        smem((LINKED, SLOTS), jnp.int32),
        smem((LINKED, SLOTS), jnp.int32),
        smem((LINKED, 2 * COLS + 1), jnp.int32),
        vmem((2, 2) + half, BF16),
        vmem((2, 2) + half, BF16),
        vmem((SUB, 2) + half, F32),
        vmem((TOP,) + half, F32),
        vmem((2, SLOTS + 1) + half, F32),
        vmem((2, COLS) + half, F32),
        vmem((COLS,) + half, F32),
        vmem((2, SUB - 1, COLS) + half, BF16),
        vmem((2, SUB - 1, 2 * COLS) + half, BF16),
        vmem((TOP, COLS) + half, BF16),
        vmem((4 * COLS,) + half, BF16),
        vmem((2, 2 * COLS) + half, BF16),
        vmem((2, COLS) + half, F32),
        vmem((2, COLS) + half, BF16),
        vmem((2, COLS) + half, BF16),
        vmem((2, COLS) + half, BF16),
        vmem((2, 7 * COLS) + half, BF16),
        vmem((2 * COLS,) + half, BF16),
        vmem((2, SUB, 2) + half, BF16),
        vmem((2, SUB, 2 * COLS) + half, BF16),
        vmem((TOP, 2) + half, BF16),
        vmem((COLS,) + half, BF16),
        vmem((2 * COLS,) + half, BF16),
        vmem((4 * COLS,) + half, BF16),
        vmem((COLS,) + half, BF16),
        vmem((COLS,) + half, BF16),
        vmem((2,) + half, F32),
        vmem((2,) + half, F32),
        vmem((TOP,) + half, F32),
        vmem((TOP,) + half, F32),
        vmem(block, BF16),
        dma((15,)),
        dma((6, LINKED)),
        pltpu.SemaphoreType.REGULAR((4,)),
        dma((10,)),
        dma((10,)),
        dma((2, SUB + TOP)),
        dma((2, SUB + TOP)),
        dma((2, SUB + TOP)),
        dma((2, SUB + TOP)),
    ]
    any_spec = pl.BlockSpec(memory_space=pl.ANY)
    vmem_spec = pl.BlockSpec(memory_space=pltpu.VMEM)
    sub, top = pl.pallas_call(
        kernel,
        out_shape=(
            jax.ShapeDtypeStruct((SUB,) + tile, F32),
            jax.ShapeDtypeStruct((TOP,) + tile, F32),
        ),
        in_specs=[any_spec] * 14,
        out_specs=(vmem_spec, vmem_spec),
        scratch_shapes=scratch,
        compiler_params=pltpu.CompilerParams(
            collective_id=0, has_side_effects=True, vmem_limit_bytes=60 * 1024 * 1024
        ),
    )(*flat)
    return hand_over(sub, top)


def solution(mesh):
    sub = P("layer", "prow", "pcol")
    top = P("prow", "pcol")
    return jax.shard_map(
        local, mesh=mesh, in_specs=(sub,) * 7 + (top,) * 7, out_specs=(sub, top), check_vma=False
    )
```

```python
import jax
import jax.numpy as jnp
from jax import lax
from jax.experimental import pallas as pl
from jax.experimental.pallas import tpu as pltpu
from jax.sharding import PartitionSpec as P

MESH = pl.DeviceIdType.MESH
F32 = jnp.float32
BF16 = jnp.bfloat16
SUB, TOP, SLOTS, COLS, SIDES, WIDTH = 5, 3, 16, 16, 32, 128
HALF = SIDES // 2
LINKED = SUB + TOP - 1
ORDER = (10, 9, 11, 6, 14, 5, 7, 13, 15, 8, 2, 1, 3, 4, 12, 0)


def dot(a, b):
    return jnp.dot(a, b, preferred_element_type=F32)


def dot_full(a, b):
    return jnp.dot(a, b, preferred_element_type=F32, precision=lax.Precision.HIGHEST)


def dot_split(a, b):
    high = a.astype(BF16)
    low = (a - high.astype(F32)).astype(BF16)
    return dot(high, b) + dot(low, b)


def wait_for(ref, sem):
    pltpu.make_async_copy(ref, ref, sem).wait()


def kernel(
    sub_rhs, sub_linv, sub_uinv, sub_lower, sub_upper, sub_src_in, sub_tgt_in,
    top_rhs, top_linv, top_uinv, top_lower, top_upper, top_src_in, top_tgt_in,
    sub_out, top_out,
    sub_src, sub_tgt, top_src, top_tgt,
    lower_0, lower, upper, linv, uinv, rhs_sub, rhs_top,
    linv_low, uinv_low, linv_other, uinv_other, pair, rhs_sub_other, rhs_top_other,
    perm, psrc, ends,
    ylow, ylow_swap, yu_sub, yu_top, sums, pend, pend_top,
    send_f, recv_f, send_ft, recv_5, recv_ft,
    halves, core_out, core_in, six,
    x_sub, x_top, send_b, recv_b, send_bt, recv_7, recv_6, recv_b5, six_in, six_out, last_out, last_in, top_mine, top_other,
    both_low, load_sem, lin_sem, group_sem, misc_recv, misc_send, rf_sem, sf_sem, rb_sem, sb_sem,
):
    l, r, c = lax.axis_index("layer"), lax.axis_index("prow"), lax.axis_index("pcol")
    high, half = l // 2, l % 2
    half_rows = pl.ds(pl.multiple_of(half * HALF, HALF), HALF)
    me = r * COLS + c

    loads = (
        (sub_lower.at[pl.ds(1, SUB - 1)], lower.at[pl.ds(1, SUB - 1)]),
        (top_lower, lower.at[pl.ds(SUB, TOP - 1)]),
        (sub_upper, upper.at[pl.ds(0, SUB)]),
        (top_upper, upper.at[pl.ds(SUB, TOP - 1)]),
        (sub_linv, linv.at[pl.ds(0, SUB)]),
        (top_linv, linv.at[pl.ds(SUB, TOP)]),
        (sub_uinv, uinv.at[pl.ds(0, SUB)]),
        (top_uinv, uinv.at[pl.ds(SUB, TOP)]),
        (sub_rhs, rhs_sub),
        (top_rhs.at[:, half_rows], rhs_top),
        (sub_src_in, sub_src),
        (sub_tgt_in, sub_tgt),
        (top_src_in, top_src),
        (top_tgt_in, top_tgt),
        (sub_lower.at[0], lower_0),
    )
    copies = [pltpu.make_async_copy(a, b, load_sem.at[i]) for i, (a, b) in enumerate(loads)]
    for i in (8, 4, 10, 11, 14, 9, 5, 12, 13, 0, 1):
        copies[i].start()

    barrier = pltpu.get_barrier_semaphore()
    for flip in (1, 2):
        pl.semaphore_signal(barrier, inc=1, device_id=(l ^ flip, r, c), device_id_type=MESH)
    pl.semaphore_signal(barrier, inc=1, device_id=(l, 1 - r, c), device_id_type=MESH)
    for i in (1, 2, 3, 4, 8, 12):
        pl.semaphore_signal(barrier, inc=1, device_id=(l, r, c ^ i), device_id_type=MESH)

    def sort_level(src, tgt, row, t):
        codes = [tgt[(*row, k)] for k in range(SLOTS)]
        rank = [jnp.int32(0)] * SLOTS
        for k in range(SLOTS):
            for j in range(k):
                before = (codes[j] <= codes[k]).astype(jnp.int32)
                rank[k] = rank[k] + before
                rank[j] = rank[j] + (1 - before)
        for i in range(SLOTS):
            slot = jnp.int32(0)
            for k in range(1, SLOTS):
                slot = slot + jnp.where(rank[k] == i, k, 0)
            perm[t, i] = slot
            psrc[t, i] = src[(*row, slot)]
        ends[t, 0] = 0
        for q in range(2 * COLS):
            count = jnp.int32(0)
            for k in range(SLOTS):
                count = count + (codes[k] <= q).astype(jnp.int32)
            ends[t, q + 1] = count

    copies[8].wait()
    copies[4].wait()
    y0 = dot_full(rhs_sub[0].reshape(SIDES, WIDTH), linv[0]).reshape(2, HALF, WIDTH)
    ylow_swap[0] = y0.astype(BF16)
    for h in range(2):
        ylow[h, r] = ylow_swap[0, h]
    pl.semaphore_wait(barrier, 9)

    def to(device, src, dst, send_sem, recv_sem):
        copy = pltpu.make_async_remote_copy(
            src_ref=src, dst_ref=dst, send_sem=send_sem, recv_sem=recv_sem, device_id=device, device_id_type=MESH
        )
        copy.start()
        return copy

    other_row = (l, 1 - r, c)
    other_core = (l ^ 1, r, c)
    other_high = (l ^ 2, r, c)

    first = to(other_row, ylow_swap.at[0], ylow_swap.at[1], misc_send.at[0], misc_recv.at[0])
    for i in (4, 8, 12):
        pl.semaphore_signal(group_sem.at[2], inc=1, device_id=(l, r, c ^ i), device_id_type=MESH)
    copies[10].wait()
    copies[11].wait()
    sort_level(sub_src, sub_tgt, (0, 0), 0)

    def lin_copy(t):
        linv_low[t - 1] = linv[t].astype(BF16)
        return to(other_row, linv_low.at[t - 1], linv_other.at[t - 1], lin_sem.at[0, t - 1], lin_sem.at[1, t - 1])

    def uin_copy(t):
        uinv_low[t] = uinv[t].astype(BF16)
        return to(other_row, uinv_low.at[t], uinv_other.at[t], lin_sem.at[2, t], lin_sem.at[3, t])

    def rhs_copy(t):
        return to(other_row, rhs_sub.at[t], rhs_sub_other.at[t - 1], lin_sem.at[4, t - 1], lin_sem.at[5, t - 1])

    def rhs_top_copy(t):
        return to(other_row, rhs_top.at[t], rhs_top_other.at[t], lin_sem.at[4, t + 4], lin_sem.at[5, t + 4])

    pl.semaphore_wait(group_sem.at[2], 3)
    pl.semaphore_signal(group_sem.at[3], inc=1, device_id=other_row, device_id_type=MESH)
    lin_copy(1)
    rhs_copy(1)
    copies[14].wait()

    def prepare_lower(t, src, row):
        wait_for(linv_other.at[t - 1], lin_sem.at[1, t - 1])
        pair[r] = linv_low[t - 1]
        pair[1 - r] = linv_other[t - 1]
        for k in range(SLOTS):
            lower[t, k] = dot(pair[src[(*row, k)]], lower[t, k]).astype(BF16)

    def prepare_upper(t, src, row):
        wait_for(uinv_other.at[t], lin_sem.at[3, t])
        pair[r] = uinv_low[t]
        pair[1 - r] = uinv_other[t]
        for k in range(SLOTS):
            upper[t, k] = dot(upper[t, k], pair[src[(*row, k)]]).astype(BF16)

    def solve_both(value, t):
        return dot_full(dot_full(value, linv[t]), uinv[t])

    streams = (1 - half, half)

    def products(h, t, block):
        total = jnp.zeros((HALF, WIDTH), F32)
        sums[h, 0] = total
        for i in range(SLOTS):
            total = total + dot(ylow[h, psrc[t, i]], block(perm[t, i]))
            sums[h, i + 1] = total

    def share(h, t, code):
        return sums[h, ends[t, code + 1]] - sums[h, ends[t, code]]

    def forward(h, t, block=None):
        products(h, t, block or (lambda k: lower[t, k]))
        for i in ORDER:
            q = c ^ i
            send_f[h, t, q] = (share(h, t, q) + pend[h, q]).astype(BF16)
            for j in (1, 0):
                if i or j:
                    to((l, r ^ j, q), send_f.at[h, t, q], recv_f.at[h, t, me], sf_sem.at[h, t], rf_sem.at[h, t + 1])
        recv_f[h, t, me] = send_f[h, t, c]

    def keep(h, t):
        for q in range(COLS):
            pend[h, q] = share(h, t, COLS + q)

    def add_up(ref, rows):
        parts = [ref[i].astype(F32) for i in range(COLS)]
        while len(parts) > 1:
            parts = [a + b for a, b in zip(parts[::2], parts[1::2])]
        return parts[0]

    def arrive(h, t, first):
        wait_for(recv_f.at[h, t - 1, pl.ds(0, 2 * COLS - 1)], rf_sem.at[h, t])
        if first:
            wait_for(rhs_sub_other.at[t - 1], lin_sem.at[5, t - 1])
        mine = rhs_sub[t, h] - add_up(recv_f.at[h, t - 1, pl.ds(r * COLS, COLS)], HALF)
        others = rhs_sub_other[t - 1, h] - add_up(recv_f.at[h, t - 1, pl.ds((1 - r) * COLS, COLS)], HALF)
        ylow[h, r] = mine.astype(BF16)
        ylow[h, 1 - r] = others.astype(BF16)
        return mine

    def finish(t, mine):
        for h, value in zip(streams, mine):
            keep(h, t)
            yu_sub[t, h] = solve_both(value, t)

    def level(t):
        mine = []
        for n, h in enumerate(streams):
            mine.append(arrive(h, t, n == 0))
            forward(h, t)
        finish(t, mine)

    pl.semaphore_wait(group_sem.at[3], 1)
    first.wait_recv()
    first.wait_send()
    for h in range(2):
        ylow[h, 1 - r] = ylow_swap[1, h]

    @pl.loop(0, COLS)
    def _(q):
        for h in range(2):
            pend[h, q] = jnp.zeros((HALF, WIDTH), F32)

    for h in streams:
        forward(h, 0, lambda k: lower_0[k])
    for i in (6, 7, 2, 3):
        copies[i].start()
    for h in streams:
        keep(h, 0)
    for i in (9, 5, 12, 13, 0, 1):
        copies[i].wait()
    lin_copy(2)
    rhs_copy(2)
    sort_level(sub_src, sub_tgt, (1, 0), 1)
    prepare_lower(1, sub_src, (1, 0))
    for i in (6, 7, 2, 3):
        copies[i].wait()
    yu_sub[0] = dot_full(y0.reshape(SIDES, WIDTH), uinv[0]).reshape(2, HALF, WIDTH)
    mine = []
    for n, h in enumerate(streams):
        mine.append(arrive(h, 1, n == 0))
        forward(h, 1)
    finish(1, mine)
    for flip in (1, 2):
        pl.semaphore_signal(group_sem.at[flip - 1], inc=1, device_id=(l ^ flip, r, c), device_id_type=MESH)
    lin_copy(3)
    rhs_copy(3)
    sort_level(sub_src, sub_tgt, (2, 0), 2)
    prepare_lower(2, sub_src, (2, 0))

    @pl.loop(2, SUB - 1)
    def _(t):
        level(t)
        lin_copy(t + 2)

        @pl.when(t == 2)
        def _():
            rhs_copy(t + 2)

        @pl.when(t == 3)
        def _():
            rhs_top_copy(0)
            rhs_top_copy(1)

        sort_level(sub_src, sub_tgt, (t + 1, 0), t + 1)
        prepare_lower(t + 1, sub_src, (t + 1, 0))

    t = SUB - 1
    theirs = arrive(1 - half, t, True)
    products(1 - half, t, lambda k: lower[t, k])
    for q in range(COLS):
        core_out[0, q] = (share(1 - half, t, q) + pend[1 - half, q]).astype(BF16)
    core_copies = [to(other_core, core_out.at[0], core_in.at[0], misc_send.at[3], misc_recv.at[3])]
    mine = arrive(half, t, False)
    products(half, t, lambda k: lower[t, k])
    for q in range(COLS):
        halves[0, q] = share(half, t, q) + pend[half, q]
    core_copies[0].wait_recv()
    pl.semaphore_wait(group_sem.at[1], 1)
    slot_5 = high * 2 * COLS + me
    for i in ORDER:
        q = c ^ i
        send_ft[0, q] = (halves[0, q] + core_in[0, q].astype(F32)).astype(BF16)
        for flip in (2, 0):
            for j in (1, 0):
                if i or j or flip:
                    to((l ^ flip, r ^ j, q), send_ft.at[0, q], recv_5.at[slot_5], sf_sem.at[0, t], rf_sem.at[0, t + 1])
    recv_5[slot_5] = send_ft[0, c]
    for q in range(COLS):
        core_out[1, q] = share(1 - half, t, COLS + q).astype(BF16)
        halves[1, q] = share(half, t, COLS + q)
    core_copies.append(to(other_core, core_out.at[1], core_in.at[1], misc_send.at[4], misc_recv.at[4]))
    lin_copy(6)
    yu_sub[t, 1 - half] = solve_both(theirs, t)
    yu_sub[t, half] = solve_both(mine, t)
    core_copies[1].wait_recv()
    six[high] = (halves[1] + core_in[1].astype(F32)).astype(BF16)
    six_copy = to(other_high, six.at[high], six.at[high], misc_send.at[5], misc_recv.at[5])
    sort_level(top_src, top_tgt, (0,), SUB)
    sort_level(top_src, top_tgt, (1,), SUB + 1)
    prepare_lower(SUB, top_src, (0,))
    six_copy.wait_recv()
    for q in range(COLS):
        pend_top[q] = six[0, q].astype(F32) + six[1, q].astype(F32)

    def arrive_top(t, mine, others):
        mine = rhs_top[t] - mine
        if t < TOP - 1:
            wait_for(rhs_top_other.at[t], lin_sem.at[5, t + 4])
            ylow[0, r] = mine.astype(BF16)
            ylow[0, 1 - r] = (rhs_top_other[t] - others).astype(BF16)
        return mine

    def forward_top(t):
        products(0, t + SUB, lambda k: lower[t + SUB, k])
        for i in ORDER:
            q = c ^ i
            value = share(0, t + SUB, q) + pend_top[q]
            send_ft[t + 1, q] = value.astype(BF16)
            for j in (1, 0) if t == 0 else (0,):
                if i or j:
                    to((l, r ^ j, q), send_ft.at[t + 1, q], recv_ft.at[t, me if t == 0 else c], sf_sem.at[0, t + SUB], rf_sem.at[0, t + SUB + 1])
        recv_ft[t, me if t == 0 else c] = send_ft[t + 1, c]
        if t == 0:
            for q in range(COLS):
                pend_top[q] = share(0, t + SUB, COLS + q)
            uin_copy(6)
        else:
            for u in (5, 4, 3):
                uin_copy(u)

    wait_for(recv_5.at[pl.ds(0, 4 * COLS - 1)], rf_sem.at[0, SUB])

    def add_up_5(row):
        return add_up(recv_5.at[pl.ds(row * COLS, COLS)], HALF) + add_up(
            recv_5.at[pl.ds((2 + row) * COLS, COLS)], HALF
        )

    value = arrive_top(0, add_up_5(r), add_up_5(1 - r))
    forward_top(0)
    prepare_lower(SUB + 1, top_src, (1,))
    yu_top[0] = solve_both(value, SUB)
    for t in (1, 2):
        wait_for(recv_ft.at[t - 1, pl.ds(0, (2 * COLS if t == 1 else COLS) - 1)], rf_sem.at[0, t + SUB])
        mine = add_up(recv_ft.at[t - 1, pl.ds(r * COLS if t == 1 else 0, COLS)], HALF)
        if t == 1:
            value = arrive_top(1, mine, add_up(recv_ft.at[t - 1, pl.ds((1 - r) * COLS, COLS)], HALF))
            forward_top(1)
            yu_top[1] = solve_both(value, SUB + 1)
            both_low[...] = dot_full(linv[7], uinv[7]).astype(BF16)
        else:
            value = arrive_top(2, mine, None)

    send_bt[2, 0] = dot_split(value, both_low[...]).astype(BF16)
    for i in ORDER:
        if i:
            to((l, r, c ^ i), send_bt.at[2, 0], recv_7.at[c], sb_sem.at[0, 7], rb_sem.at[0, 7])
    recv_7[c] = send_bt[2, 0]
    top_mine[2] = dot_full(dot_full(value, linv[7]), uinv[7])
    for u in (2, 1, 0):
        uin_copy(u)
    prepare_upper(6, top_src, (1,))
    wait_for(recv_7.at[pl.ds(0, COLS - 1)], rb_sem.at[0, 7])
    x_top[pl.ds(COLS, COLS)] = recv_7[...]

    def down(t, load, src, row):
        total = None
        for k in range(SLOTS):
            value = dot(load(k), upper[t, k])
            taken = value * src[(*row, k)].astype(F32)
            total = value if total is None else total + value
            second = taken if k == 0 else second + taken
        at_first = r == 0
        parts = (total - second, second)
        return jnp.where(at_first, parts[0], parts[1]), jnp.where(at_first, parts[1], parts[0])

    mine, others = down(6, lambda k: x_top[COLS + top_tgt[1, k] % COLS], top_src, (1,))
    a, b = yu_top[1] - mine, -others
    send_bt[1, 0] = a.astype(BF16)
    send_bt[1, 1] = b.astype(BF16)
    for i in ORDER:
        to((l, 1 - r, c ^ i), send_bt.at[1, 1], recv_6.at[COLS + c], sb_sem.at[0, 6], rb_sem.at[0, 6])
        if i:
            to((l, r, c ^ i), send_bt.at[1, 0], recv_6.at[c], sb_sem.at[0, 6], rb_sem.at[0, 6])
    recv_6[c] = send_bt[1, 0]
    top_mine[1] = a
    prepare_upper(5, top_src, (0,))
    wait_for(recv_6.at[pl.ds(0, 2 * COLS - 1)], rb_sem.at[0, 6])
    for q in range(COLS):
        x_top[q] = (recv_6[q].astype(F32) + recv_6[COLS + q].astype(F32)).astype(BF16)
    top_mine[1] = top_mine[1] + recv_6[COLS + c].astype(F32)
    six_out[...] = x_top[pl.ds(0, COLS)]
    x6_copy = to(other_core, six_out, six_in, misc_send.at[7], misc_recv.at[7])

    mine, others = down(5, lambda k: x_top[top_tgt[0, k]], top_src, (0,))
    a, b = yu_top[0] - mine, -others
    send_bt[0, 0] = a.astype(BF16)
    send_bt[0, 1] = b.astype(BF16)
    pl.semaphore_wait(group_sem.at[0], 1)
    slot_a = half * 2 * COLS + c
    for i in ORDER:
        for flip in (1, 0):
            to((l ^ flip, 1 - r, c ^ i), send_bt.at[0, 1], recv_b5.at[slot_a + COLS], sb_sem.at[0, 5], rb_sem.at[0, 5])
            if i or flip:
                to((l ^ flip, r, c ^ i), send_bt.at[0, 0], recv_b5.at[slot_a], sb_sem.at[0, 5], rb_sem.at[0, 5])
    recv_b5[slot_a] = send_bt[0, 0]
    top_mine[0] = a
    prepare_upper(4, sub_src, (4, 0))
    x6_copy.wait_recv()
    for q in range(COLS):
        x_sub[half, 6 * COLS + q] = x_top[q]
        x_sub[1 - half, 6 * COLS + q] = six_in[q]
    wait_for(recv_b5.at[pl.ds(0, 4 * COLS - 1)], rb_sem.at[0, 5])
    for q in range(COLS):
        for h in range(2):
            x_sub[h, 5 * COLS + q] = (
                recv_b5[h * 2 * COLS + q].astype(F32) + recv_b5[h * 2 * COLS + COLS + q].astype(F32)
            ).astype(BF16)
    top_mine[0] = top_mine[0] + recv_b5[slot_a + COLS].astype(F32)
    top_copy = to(other_core, top_mine, top_other, misc_send.at[6], misc_recv.at[6])

    def down_sub(h, t):
        return down(t, lambda k: x_sub[h, (t + 1) * COLS + sub_tgt[t, 0, k]], sub_src, (t, 0))

    def climb_down(h, t):
        mine, others = down_sub(h, t)
        a, b = yu_sub[t, h] - mine, -others
        send_b[h, t, 0] = a.astype(BF16)
        send_b[h, t, 1] = b.astype(BF16)
        for i in ORDER:
            to((l, 1 - r, c ^ i), send_b.at[h, t, 1], recv_b.at[h, t, COLS + c], sb_sem.at[h, t], rb_sem.at[h, t])
            if i:
                to((l, r, c ^ i), send_b.at[h, t, 0], recv_b.at[h, t, c], sb_sem.at[h, t], rb_sem.at[h, t])
        recv_b[h, t, c] = send_b[h, t, 0]
        return a

    def solved(h, t):
        wait_for(recv_b.at[h, t, pl.ds(0, 2 * COLS - 1)], rb_sem.at[h, t])
        for q in range(COLS):
            x_sub[h, t * COLS + q] = (recv_b[h, t, q].astype(F32) + recv_b[h, t, COLS + q].astype(F32)).astype(BF16)

    def put_out(h, t, mine):
        rows = pl.ds(pl.multiple_of(h * HALF, HALF), HALF)
        sub_out[t, rows] = mine + recv_b[h, t, COLS + c].astype(F32)

    kept = [climb_down(h, SUB - 1) for h in streams]
    prepare_upper(SUB - 2, sub_src, (SUB - 2, 0))

    def descend(step, kept):
        t = SUB - 2 - step
        later = []
        for h in streams:
            solved(h, t + 1)
            later.append(climb_down(h, t))
        for h, value in zip(streams, kept):
            put_out(h, t + 1, value)
        prepare_upper(t - 1, sub_src, (t - 1, 0))
        return tuple(later)

    kept = lax.fori_loop(0, SUB - 2, descend, tuple(kept))
    mine, last = [], []
    for n, h in enumerate(streams):
        solved(h, 1)
        value, others = down_sub(h, 0)
        mine.append(yu_sub[0, h] - value)
        last_out[h] = -others
        last.append(to(other_row, last_out.at[h], last_in.at[h], misc_send.at[8 + n], misc_recv.at[8 + n]))
    for h, value in zip(streams, kept):
        put_out(h, 1, value)
    top_copy.wait_recv()
    for t in range(TOP):
        top_out[t, half_rows] = top_mine[t]
        top_out[t, pl.ds(pl.multiple_of((1 - half) * HALF, HALF), HALF)] = top_other[t]

    for copy in (*core_copies, six_copy, x6_copy, top_copy):
        copy.wait_send()
    for t in range(LINKED):
        wait_for(uinv_other.at[t], lin_sem.at[2, t])
    for t in range(6):
        wait_for(linv_other.at[t], lin_sem.at[0, t])
        wait_for(rhs_sub_other.at[t] if t < 4 else rhs_top_other.at[t - 4], lin_sem.at[4, t])
    for t in range(SUB - 1):
        for h in range(2):
            wait_for(recv_f.at[h, t, pl.ds(0, 2 * COLS - 1)], sf_sem.at[h, t])
    wait_for(recv_5.at[pl.ds(0, 4 * COLS - 1)], sf_sem.at[0, 4])
    wait_for(recv_ft.at[0, pl.ds(0, 2 * COLS - 1)], sf_sem.at[0, 5])
    wait_for(recv_ft.at[1, pl.ds(0, COLS - 1)], sf_sem.at[0, 6])
    wait_for(recv_7.at[pl.ds(0, COLS - 1)], sb_sem.at[0, 7])
    wait_for(recv_6.at[pl.ds(0, 2 * COLS - 1)], sb_sem.at[0, 6])
    wait_for(recv_b5.at[pl.ds(0, 4 * COLS - 1)], sb_sem.at[0, 5])
    for t in range(1, SUB):
        for h in range(2):
            wait_for(recv_b.at[h, t, pl.ds(0, 2 * COLS - 1)], sb_sem.at[h, t])
    for h, value, copy in zip(streams, mine, last):
        copy.wait_send()
        copy.wait_recv()
        rows = pl.ds(pl.multiple_of(h * HALF, HALF), HALF)
        sub_out[0, rows] = value + last_in[h]


def hand_over(sub, top):
    def body(sub_in, top_in, sub_res, top_res, sems):
        copies = [
            pltpu.make_async_copy(sub_in, sub_res.at[0, 0, 0], sems.at[0]),
            pltpu.make_async_copy(top_in, top_res.at[0, 0], sems.at[1]),
        ]
        for copy in copies:
            copy.start()
        for copy in copies:
            copy.wait()

    any_spec = pl.BlockSpec(memory_space=pl.ANY)
    return pl.pallas_call(
        body,
        out_shape=(
            jax.ShapeDtypeStruct((1, 1, 1) + sub.shape, F32),
            jax.ShapeDtypeStruct((1, 1) + top.shape, F32),
        ),
        in_specs=[any_spec] * 2,
        out_specs=[any_spec] * 2,
        scratch_shapes=[pltpu.SemaphoreType.DMA((2,))],
    )(pltpu.with_memory_space_constraint(sub, pltpu.VMEM), pltpu.with_memory_space_constraint(top, pltpu.VMEM))


def local(*args):
    flat = [a.reshape(a.shape[3:] if i < 7 else a.shape[2:]) for i, a in enumerate(args)]
    flat[0] = args[0].reshape(SUB, 2, HALF, WIDTH)
    flat[5], flat[6] = (a.reshape(SUB, 1, SLOTS) for a in args[5:7])
    flat = [pltpu.with_memory_space_constraint(a, pltpu.HBM) for a in flat]
    vmem, smem, dma = pltpu.VMEM, pltpu.SMEM, pltpu.SemaphoreType.DMA
    tile = (SIDES, WIDTH)
    half = (HALF, WIDTH)
    block = (WIDTH, WIDTH)
    scratch = [
        smem((SUB, 1, SLOTS), jnp.int32),
        smem((SUB, 1, SLOTS), jnp.int32),
        smem((TOP - 1, SLOTS), jnp.int32),
        smem((TOP - 1, SLOTS), jnp.int32),
        vmem((SLOTS,) + block, BF16),
        vmem((LINKED, SLOTS) + block, BF16),
        vmem((LINKED, SLOTS) + block, BF16),
        vmem((SUB + TOP,) + block, F32),
        vmem((SUB + TOP,) + block, F32),
        vmem((SUB, 2) + half, F32),
        vmem((TOP,) + half, F32),
        vmem((6,) + block, BF16),
        vmem((LINKED,) + block, BF16),
        vmem((6,) + block, BF16),
        vmem((LINKED,) + block, BF16),
        vmem((2,) + block, BF16),
        vmem((SUB - 1, 2) + half, F32),
        vmem((2,) + half, F32),
        smem((LINKED, SLOTS), jnp.int32),
        smem((LINKED, SLOTS), jnp.int32),
        smem((LINKED, 2 * COLS + 1), jnp.int32),
        vmem((2, 2) + half, BF16),
        vmem((2, 2) + half, BF16),
        vmem((SUB, 2) + half, F32),
        vmem((TOP,) + half, F32),
        vmem((2, SLOTS + 1) + half, F32),
        vmem((2, COLS) + half, F32),
        vmem((COLS,) + half, F32),
        vmem((2, SUB - 1, COLS) + half, BF16),
        vmem((2, SUB - 1, 2 * COLS) + half, BF16),
        vmem((TOP, COLS) + half, BF16),
        vmem((4 * COLS,) + half, BF16),
        vmem((2, 2 * COLS) + half, BF16),
        vmem((2, COLS) + half, F32),
        vmem((2, COLS) + half, BF16),
        vmem((2, COLS) + half, BF16),
        vmem((2, COLS) + half, BF16),
        vmem((2, 7 * COLS) + half, BF16),
        vmem((2 * COLS,) + half, BF16),
        vmem((2, SUB, 2) + half, BF16),
        vmem((2, SUB, 2 * COLS) + half, BF16),
        vmem((TOP, 2) + half, BF16),
        vmem((COLS,) + half, BF16),
        vmem((2 * COLS,) + half, BF16),
        vmem((4 * COLS,) + half, BF16),
        vmem((COLS,) + half, BF16),
        vmem((COLS,) + half, BF16),
        vmem((2,) + half, F32),
        vmem((2,) + half, F32),
        vmem((TOP,) + half, F32),
        vmem((TOP,) + half, F32),
        vmem(block, BF16),
        dma((15,)),
        dma((6, LINKED)),
        pltpu.SemaphoreType.REGULAR((4,)),
        dma((10,)),
        dma((10,)),
        dma((2, SUB + TOP)),
        dma((2, SUB + TOP)),
        dma((2, SUB + TOP)),
        dma((2, SUB + TOP)),
    ]
    any_spec = pl.BlockSpec(memory_space=pl.ANY)
    vmem_spec = pl.BlockSpec(memory_space=pltpu.VMEM)
    sub, top = pl.pallas_call(
        kernel,
        out_shape=(
            jax.ShapeDtypeStruct((SUB,) + tile, F32),
            jax.ShapeDtypeStruct((TOP,) + tile, F32),
        ),
        in_specs=[any_spec] * 14,
        out_specs=(vmem_spec, vmem_spec),
        scratch_shapes=scratch,
        compiler_params=pltpu.CompilerParams(
            collective_id=0, has_side_effects=True, vmem_limit_bytes=48 * 1024 * 1024
        ),
    )(*flat)
    return hand_over(sub, top)


def solution(mesh):
    sub = P("layer", "prow", "pcol")
    top = P("prow", "pcol")
    return jax.shard_map(
        local, mesh=mesh, in_specs=(sub,) * 7 + (top,) * 7, out_specs=(sub, top), check_vma=False
    )
```

```python
import jax
import jax.numpy as jnp
from jax import lax
from jax.experimental import pallas as pl
from jax.experimental.pallas import tpu as pltpu
from jax.sharding import PartitionSpec as P

MESH = pl.DeviceIdType.MESH
F32 = jnp.float32
BF16 = jnp.bfloat16
SUB, TOP, SLOTS, COLS, SIDES, WIDTH = 5, 3, 16, 16, 32, 128
HALF = SIDES // 2
LINKED = SUB + TOP - 1
ORDER = (10, 11, 14, 9, 6, 15, 7, 13, 5, 8, 2, 3, 12, 1, 4, 0)


def dot(a, b):
    return jnp.dot(a, b, preferred_element_type=F32)


def dot_full(a, b):
    return jnp.dot(a, b, preferred_element_type=F32, precision=lax.Precision.HIGHEST)


def dot_split(a, b):
    high = a.astype(BF16)
    low = (a - high.astype(F32)).astype(BF16)
    return dot(high, b) + dot(low, b)


def wait_for(ref, sem):
    pltpu.make_async_copy(ref, ref, sem).wait()


def kernel(
    sub_rhs, sub_linv, sub_uinv, sub_lower, sub_upper, sub_src_in, sub_tgt_in,
    top_rhs, top_linv, top_uinv, top_lower, top_upper, top_src_in, top_tgt_in,
    sub_out, top_out,
    sub_src, sub_tgt, top_src, top_tgt,
    lower_0, lower, upper, linv, uinv, rhs_sub, rhs_top,
    linv_low, uinv_low, linv_other, uinv_other, pair, rhs_sub_other, rhs_top_other,
    perm, psrc, ends,
    ylow, ylow_swap, yu_sub, yu_top, sums, pend, pend_top,
    send_f, recv_f, send_ft, recv_5, recv_ft,
    halves, core_out, core_in, six,
    x_sub, x_top, send_b, recv_b, send_bt, recv_7, recv_6, recv_b5, six_in, six_out, last_out, last_in, top_mine, top_other,
    both_low, load_sem, lin_sem, group_sem, misc_recv, misc_send, rf_sem, sf_sem, rb_sem, sb_sem,
):
    l, r, c = lax.axis_index("layer"), lax.axis_index("prow"), lax.axis_index("pcol")
    high, half = l // 2, l % 2
    half_rows = pl.ds(pl.multiple_of(half * HALF, HALF), HALF)
    me = r * COLS + c

    loads = (
        (sub_lower.at[pl.ds(1, SUB - 1)], lower.at[pl.ds(1, SUB - 1)]),
        (top_lower, lower.at[pl.ds(SUB, TOP - 1)]),
        (sub_upper, upper.at[pl.ds(0, SUB)]),
        (top_upper, upper.at[pl.ds(SUB, TOP - 1)]),
        (sub_linv, linv.at[pl.ds(0, SUB)]),
        (top_linv, linv.at[pl.ds(SUB, TOP)]),
        (sub_uinv, uinv.at[pl.ds(0, SUB)]),
        (top_uinv, uinv.at[pl.ds(SUB, TOP)]),
        (sub_rhs, rhs_sub),
        (top_rhs.at[:, half_rows], rhs_top),
        (sub_src_in, sub_src),
        (sub_tgt_in, sub_tgt),
        (top_src_in, top_src),
        (top_tgt_in, top_tgt),
        (sub_lower.at[0], lower_0),
    )
    copies = [pltpu.make_async_copy(a, b, load_sem.at[i]) for i, (a, b) in enumerate(loads)]
    for i in (8, 4, 10, 11, 14, 9, 5, 12, 13, 0, 1):
        copies[i].start()

    barrier = pltpu.get_barrier_semaphore()
    for flip in (1, 2):
        pl.semaphore_signal(barrier, inc=1, device_id=(l ^ flip, r, c), device_id_type=MESH)
    pl.semaphore_signal(barrier, inc=1, device_id=(l, 1 - r, c), device_id_type=MESH)
    for i in (1, 2, 3, 4, 8, 12):
        pl.semaphore_signal(barrier, inc=1, device_id=(l, r, c ^ i), device_id_type=MESH)

    def sort_level(src, tgt, row, t):
        codes = [tgt[(*row, k)] for k in range(SLOTS)]
        rank = [jnp.int32(0)] * SLOTS
        for k in range(SLOTS):
            for j in range(k):
                before = (codes[j] <= codes[k]).astype(jnp.int32)
                rank[k] = rank[k] + before
                rank[j] = rank[j] + (1 - before)
        for i in range(SLOTS):
            slot = jnp.int32(0)
            for k in range(1, SLOTS):
                slot = slot + jnp.where(rank[k] == i, k, 0)
            perm[t, i] = slot
            psrc[t, i] = src[(*row, slot)]
        ends[t, 0] = 0
        for q in range(2 * COLS):
            count = jnp.int32(0)
            for k in range(SLOTS):
                count = count + (codes[k] <= q).astype(jnp.int32)
            ends[t, q + 1] = count

    copies[8].wait()
    copies[4].wait()
    y0 = dot_full(rhs_sub[0].reshape(SIDES, WIDTH), linv[0]).reshape(2, HALF, WIDTH)
    ylow_swap[0] = y0.astype(BF16)
    for h in range(2):
        ylow[h, r] = ylow_swap[0, h]
    pl.semaphore_wait(barrier, 9)

    def to(device, src, dst, send_sem, recv_sem):
        copy = pltpu.make_async_remote_copy(
            src_ref=src, dst_ref=dst, send_sem=send_sem, recv_sem=recv_sem, device_id=device, device_id_type=MESH
        )
        copy.start()
        return copy

    other_row = (l, 1 - r, c)
    other_core = (l ^ 1, r, c)
    other_high = (l ^ 2, r, c)

    first = to(other_row, ylow_swap.at[0], ylow_swap.at[1], misc_send.at[0], misc_recv.at[0])
    for i in (4, 8, 12):
        pl.semaphore_signal(group_sem.at[2], inc=1, device_id=(l, r, c ^ i), device_id_type=MESH)
    copies[10].wait()
    copies[11].wait()
    sort_level(sub_src, sub_tgt, (0, 0), 0)

    def lin_copy(t):
        linv_low[t - 1] = linv[t].astype(BF16)
        return to(other_row, linv_low.at[t - 1], linv_other.at[t - 1], lin_sem.at[0, t - 1], lin_sem.at[1, t - 1])

    def uin_copy(t):
        uinv_low[t] = uinv[t].astype(BF16)
        return to(other_row, uinv_low.at[t], uinv_other.at[t], lin_sem.at[2, t], lin_sem.at[3, t])

    def rhs_copy(t):
        return to(other_row, rhs_sub.at[t], rhs_sub_other.at[t - 1], lin_sem.at[4, t - 1], lin_sem.at[5, t - 1])

    def rhs_top_copy(t):
        return to(other_row, rhs_top.at[t], rhs_top_other.at[t], lin_sem.at[4, t + 4], lin_sem.at[5, t + 4])

    pl.semaphore_wait(group_sem.at[2], 3)
    pl.semaphore_signal(group_sem.at[3], inc=1, device_id=other_row, device_id_type=MESH)
    lin_copy(1)
    rhs_copy(1)
    copies[14].wait()

    def prepare_lower(t, src, row):
        wait_for(linv_other.at[t - 1], lin_sem.at[1, t - 1])
        pair[r] = linv_low[t - 1]
        pair[1 - r] = linv_other[t - 1]
        for k in range(SLOTS):
            lower[t, k] = dot(pair[src[(*row, k)]], lower[t, k]).astype(BF16)

    def prepare_upper(t, src, row):
        wait_for(uinv_other.at[t], lin_sem.at[3, t])
        pair[r] = uinv_low[t]
        pair[1 - r] = uinv_other[t]
        for k in range(SLOTS):
            upper[t, k] = dot(upper[t, k], pair[src[(*row, k)]]).astype(BF16)

    def solve_both(value, t):
        return dot_full(dot_full(value, linv[t]), uinv[t])

    streams = (1 - half, half)

    def products(h, t, block):
        total = jnp.zeros((HALF, WIDTH), F32)
        sums[h, 0] = total
        for i in range(SLOTS):
            total = total + dot(ylow[h, psrc[t, i]], block(perm[t, i]))
            sums[h, i + 1] = total

    def share(h, t, code):
        return sums[h, ends[t, code + 1]] - sums[h, ends[t, code]]

    def forward(h, t, block=None):
        products(h, t, block or (lambda k: lower[t, k]))
        for i in ORDER:
            q = c ^ i
            send_f[h, t, q] = (share(h, t, q) + pend[h, q]).astype(BF16)
            for j in (1, 0):
                if i or j:
                    to((l, r ^ j, q), send_f.at[h, t, q], recv_f.at[h, t, me], sf_sem.at[h, t], rf_sem.at[h, t + 1])
        recv_f[h, t, me] = send_f[h, t, c]

    def keep(h, t):
        for q in range(COLS):
            pend[h, q] = share(h, t, COLS + q)

    def add_up(ref, rows):
        parts = [ref[i].astype(F32) for i in range(COLS)]
        while len(parts) > 1:
            parts = [a + b for a, b in zip(parts[::2], parts[1::2])]
        return parts[0]

    def arrive(h, t, first):
        wait_for(recv_f.at[h, t - 1, pl.ds(0, 2 * COLS - 1)], rf_sem.at[h, t])
        if first:
            wait_for(rhs_sub_other.at[t - 1], lin_sem.at[5, t - 1])
        mine = rhs_sub[t, h] - add_up(recv_f.at[h, t - 1, pl.ds(r * COLS, COLS)], HALF)
        others = rhs_sub_other[t - 1, h] - add_up(recv_f.at[h, t - 1, pl.ds((1 - r) * COLS, COLS)], HALF)
        ylow[h, r] = mine.astype(BF16)
        ylow[h, 1 - r] = others.astype(BF16)
        return mine

    def finish(t, mine):
        for h, value in zip(streams, mine):
            keep(h, t)
            yu_sub[t, h] = solve_both(value, t)

    def early(t):
        lin_copy(t + 2)

        @pl.when(t == 2)
        def _():
            rhs_copy(t + 2)

        @pl.when(t == 3)
        def _():
            rhs_top_copy(0)
            rhs_top_copy(1)

    def level(t):
        mine = []
        for n, h in enumerate(streams):
            mine.append(arrive(h, t, n == 0))
            forward(h, t)
            if n == 0:
                early(t)
        finish(t, mine)

    pl.semaphore_wait(group_sem.at[3], 1)
    first.wait_recv()
    first.wait_send()
    for h in range(2):
        ylow[h, 1 - r] = ylow_swap[1, h]

    @pl.loop(0, COLS)
    def _(q):
        for h in range(2):
            pend[h, q] = jnp.zeros((HALF, WIDTH), F32)

    for h in streams:
        forward(h, 0, lambda k: lower_0[k])
    for i in (6, 7, 2, 3):
        copies[i].start()
    for h in streams:
        keep(h, 0)
    for i in (9, 5, 12, 13, 0, 1):
        copies[i].wait()
    lin_copy(2)
    rhs_copy(2)
    sort_level(sub_src, sub_tgt, (1, 0), 1)
    prepare_lower(1, sub_src, (1, 0))
    for i in (6, 7, 2, 3):
        copies[i].wait()
    yu_sub[0] = dot_full(y0.reshape(SIDES, WIDTH), uinv[0]).reshape(2, HALF, WIDTH)
    mine = []
    for n, h in enumerate(streams):
        mine.append(arrive(h, 1, n == 0))
        forward(h, 1)
        if n == 0:
            lin_copy(3)
            rhs_copy(3)
    finish(1, mine)
    for flip in (1, 2):
        pl.semaphore_signal(group_sem.at[flip - 1], inc=1, device_id=(l ^ flip, r, c), device_id_type=MESH)
    sort_level(sub_src, sub_tgt, (2, 0), 2)
    prepare_lower(2, sub_src, (2, 0))

    @pl.loop(2, SUB - 1)
    def _(t):
        level(t)
        sort_level(sub_src, sub_tgt, (t + 1, 0), t + 1)
        prepare_lower(t + 1, sub_src, (t + 1, 0))

    t = SUB - 1
    theirs = arrive(1 - half, t, True)
    products(1 - half, t, lambda k: lower[t, k])
    for q in range(COLS):
        core_out[0, q] = (share(1 - half, t, q) + pend[1 - half, q]).astype(BF16)
    core_copies = [to(other_core, core_out.at[0], core_in.at[0], misc_send.at[3], misc_recv.at[3])]
    mine = arrive(half, t, False)
    products(half, t, lambda k: lower[t, k])
    for q in range(COLS):
        halves[0, q] = share(half, t, q) + pend[half, q]
    core_copies[0].wait_recv()
    pl.semaphore_wait(group_sem.at[1], 1)
    slot_5 = high * 2 * COLS + me
    for i in ORDER:
        q = c ^ i
        send_ft[0, q] = (halves[0, q] + core_in[0, q].astype(F32)).astype(BF16)
        for flip in (2, 0):
            for j in (1, 0):
                if i or j or flip:
                    to((l ^ flip, r ^ j, q), send_ft.at[0, q], recv_5.at[slot_5], sf_sem.at[0, t], rf_sem.at[0, t + 1])
    recv_5[slot_5] = send_ft[0, c]
    for q in range(COLS):
        core_out[1, q] = share(1 - half, t, COLS + q).astype(BF16)
        halves[1, q] = share(half, t, COLS + q)
    core_copies.append(to(other_core, core_out.at[1], core_in.at[1], misc_send.at[4], misc_recv.at[4]))
    lin_copy(6)
    yu_sub[t, 1 - half] = solve_both(theirs, t)
    yu_sub[t, half] = solve_both(mine, t)
    core_copies[1].wait_recv()
    six[high] = (halves[1] + core_in[1].astype(F32)).astype(BF16)
    six_copy = to(other_high, six.at[high], six.at[high], misc_send.at[5], misc_recv.at[5])
    sort_level(top_src, top_tgt, (0,), SUB)
    sort_level(top_src, top_tgt, (1,), SUB + 1)
    prepare_lower(SUB, top_src, (0,))
    six_copy.wait_recv()
    for q in range(COLS):
        pend_top[q] = six[0, q].astype(F32) + six[1, q].astype(F32)

    def arrive_top(t, mine, others):
        mine = rhs_top[t] - mine
        if t < TOP - 1:
            wait_for(rhs_top_other.at[t], lin_sem.at[5, t + 4])
            ylow[0, r] = mine.astype(BF16)
            ylow[0, 1 - r] = (rhs_top_other[t] - others).astype(BF16)
        return mine

    def forward_top(t):
        products(0, t + SUB, lambda k: lower[t + SUB, k])
        for i in ORDER:
            q = c ^ i
            value = share(0, t + SUB, q) + pend_top[q]
            send_ft[t + 1, q] = value.astype(BF16)
            for j in (1, 0) if t == 0 else (0,):
                if i or j:
                    to((l, r ^ j, q), send_ft.at[t + 1, q], recv_ft.at[t, me if t == 0 else c], sf_sem.at[0, t + SUB], rf_sem.at[0, t + SUB + 1])
        recv_ft[t, me if t == 0 else c] = send_ft[t + 1, c]
        if t == 0:
            for q in range(COLS):
                pend_top[q] = share(0, t + SUB, COLS + q)
            uin_copy(6)
        else:
            for u in (5, 4, 3):
                uin_copy(u)

    wait_for(recv_5.at[pl.ds(0, 4 * COLS - 1)], rf_sem.at[0, SUB])

    def add_up_5(row):
        return add_up(recv_5.at[pl.ds(row * COLS, COLS)], HALF) + add_up(
            recv_5.at[pl.ds((2 + row) * COLS, COLS)], HALF
        )

    value = arrive_top(0, add_up_5(r), add_up_5(1 - r))
    forward_top(0)
    prepare_lower(SUB + 1, top_src, (1,))
    yu_top[0] = solve_both(value, SUB)
    for t in (1, 2):
        wait_for(recv_ft.at[t - 1, pl.ds(0, (2 * COLS if t == 1 else COLS) - 1)], rf_sem.at[0, t + SUB])
        mine = add_up(recv_ft.at[t - 1, pl.ds(r * COLS if t == 1 else 0, COLS)], HALF)
        if t == 1:
            value = arrive_top(1, mine, add_up(recv_ft.at[t - 1, pl.ds((1 - r) * COLS, COLS)], HALF))
            forward_top(1)
            yu_top[1] = solve_both(value, SUB + 1)
            both_low[...] = dot_full(linv[7], uinv[7]).astype(BF16)
        else:
            value = arrive_top(2, mine, None)

    send_bt[2, 0] = dot_split(value, both_low[...]).astype(BF16)
    for i in ORDER:
        if i:
            to((l, r, c ^ i), send_bt.at[2, 0], recv_7.at[c], sb_sem.at[0, 7], rb_sem.at[0, 7])
    recv_7[c] = send_bt[2, 0]
    top_mine[2] = dot_full(dot_full(value, linv[7]), uinv[7])
    for u in (2, 1, 0):
        uin_copy(u)
    prepare_upper(6, top_src, (1,))
    wait_for(recv_7.at[pl.ds(0, COLS - 1)], rb_sem.at[0, 7])
    x_top[pl.ds(COLS, COLS)] = recv_7[...]

    def down(t, load, src, row):
        total = None
        for k in range(SLOTS):
            value = dot(load(k), upper[t, k])
            taken = value * src[(*row, k)].astype(F32)
            total = value if total is None else total + value
            second = taken if k == 0 else second + taken
        at_first = r == 0
        parts = (total - second, second)
        return jnp.where(at_first, parts[0], parts[1]), jnp.where(at_first, parts[1], parts[0])

    mine, others = down(6, lambda k: x_top[COLS + top_tgt[1, k] % COLS], top_src, (1,))
    a, b = yu_top[1] - mine, -others
    send_bt[1, 0] = a.astype(BF16)
    send_bt[1, 1] = b.astype(BF16)
    for i in ORDER:
        to((l, 1 - r, c ^ i), send_bt.at[1, 1], recv_6.at[COLS + c], sb_sem.at[0, 6], rb_sem.at[0, 6])
        if i:
            to((l, r, c ^ i), send_bt.at[1, 0], recv_6.at[c], sb_sem.at[0, 6], rb_sem.at[0, 6])
    recv_6[c] = send_bt[1, 0]
    top_mine[1] = a
    prepare_upper(5, top_src, (0,))
    wait_for(recv_6.at[pl.ds(0, 2 * COLS - 1)], rb_sem.at[0, 6])
    for q in range(COLS):
        x_top[q] = (recv_6[q].astype(F32) + recv_6[COLS + q].astype(F32)).astype(BF16)
    top_mine[1] = top_mine[1] + recv_6[COLS + c].astype(F32)
    six_out[...] = x_top[pl.ds(0, COLS)]
    x6_copy = to(other_core, six_out, six_in, misc_send.at[7], misc_recv.at[7])

    mine, others = down(5, lambda k: x_top[top_tgt[0, k]], top_src, (0,))
    a, b = yu_top[0] - mine, -others
    send_bt[0, 0] = a.astype(BF16)
    send_bt[0, 1] = b.astype(BF16)
    pl.semaphore_wait(group_sem.at[0], 1)
    slot_a = half * 2 * COLS + c
    for i in ORDER:
        for flip in (1, 0):
            to((l ^ flip, 1 - r, c ^ i), send_bt.at[0, 1], recv_b5.at[slot_a + COLS], sb_sem.at[0, 5], rb_sem.at[0, 5])
            if i or flip:
                to((l ^ flip, r, c ^ i), send_bt.at[0, 0], recv_b5.at[slot_a], sb_sem.at[0, 5], rb_sem.at[0, 5])
    recv_b5[slot_a] = send_bt[0, 0]
    top_mine[0] = a
    prepare_upper(4, sub_src, (4, 0))
    x6_copy.wait_recv()
    for q in range(COLS):
        x_sub[half, 6 * COLS + q] = x_top[q]
        x_sub[1 - half, 6 * COLS + q] = six_in[q]
    wait_for(recv_b5.at[pl.ds(0, 4 * COLS - 1)], rb_sem.at[0, 5])
    for q in range(COLS):
        for h in range(2):
            x_sub[h, 5 * COLS + q] = (
                recv_b5[h * 2 * COLS + q].astype(F32) + recv_b5[h * 2 * COLS + COLS + q].astype(F32)
            ).astype(BF16)
    top_mine[0] = top_mine[0] + recv_b5[slot_a + COLS].astype(F32)
    top_copy = to(other_core, top_mine, top_other, misc_send.at[6], misc_recv.at[6])

    def down_sub(h, t):
        return down(t, lambda k: x_sub[h, (t + 1) * COLS + sub_tgt[t, 0, k]], sub_src, (t, 0))

    def climb_down(h, t):
        mine, others = down_sub(h, t)
        a, b = yu_sub[t, h] - mine, -others
        send_b[h, t, 0] = a.astype(BF16)
        send_b[h, t, 1] = b.astype(BF16)
        for i in ORDER:
            to((l, 1 - r, c ^ i), send_b.at[h, t, 1], recv_b.at[h, t, COLS + c], sb_sem.at[h, t], rb_sem.at[h, t])
            if i:
                to((l, r, c ^ i), send_b.at[h, t, 0], recv_b.at[h, t, c], sb_sem.at[h, t], rb_sem.at[h, t])
        recv_b[h, t, c] = send_b[h, t, 0]
        return a

    def solved(h, t):
        wait_for(recv_b.at[h, t, pl.ds(0, 2 * COLS - 1)], rb_sem.at[h, t])
        for q in range(COLS):
            x_sub[h, t * COLS + q] = (recv_b[h, t, q].astype(F32) + recv_b[h, t, COLS + q].astype(F32)).astype(BF16)

    def put_out(h, t, mine):
        rows = pl.ds(pl.multiple_of(h * HALF, HALF), HALF)
        sub_out[t, rows] = mine + recv_b[h, t, COLS + c].astype(F32)

    kept = [climb_down(h, SUB - 1) for h in streams]
    prepare_upper(SUB - 2, sub_src, (SUB - 2, 0))

    def descend(step, kept):
        t = SUB - 2 - step
        later = []
        for h in streams:
            solved(h, t + 1)
            later.append(climb_down(h, t))
        for h, value in zip(streams, kept):
            put_out(h, t + 1, value)
        prepare_upper(t - 1, sub_src, (t - 1, 0))
        return tuple(later)

    kept = lax.fori_loop(0, SUB - 2, descend, tuple(kept))
    mine, last = [], []
    for n, h in enumerate(streams):
        solved(h, 1)
        value, others = down_sub(h, 0)
        mine.append(yu_sub[0, h] - value)
        last_out[h] = -others
        last.append(to(other_row, last_out.at[h], last_in.at[h], misc_send.at[8 + n], misc_recv.at[8 + n]))
    for h, value in zip(streams, kept):
        put_out(h, 1, value)
    top_copy.wait_recv()
    for t in range(TOP):
        top_out[t, half_rows] = top_mine[t]
        top_out[t, pl.ds(pl.multiple_of((1 - half) * HALF, HALF), HALF)] = top_other[t]

    for copy in (*core_copies, six_copy, x6_copy, top_copy):
        copy.wait_send()
    for t in range(LINKED):
        wait_for(uinv_other.at[t], lin_sem.at[2, t])
    for t in range(6):
        wait_for(linv_other.at[t], lin_sem.at[0, t])
        wait_for(rhs_sub_other.at[t] if t < 4 else rhs_top_other.at[t - 4], lin_sem.at[4, t])
    for t in range(SUB - 1):
        for h in range(2):
            wait_for(recv_f.at[h, t, pl.ds(0, 2 * COLS - 1)], sf_sem.at[h, t])
    wait_for(recv_5.at[pl.ds(0, 4 * COLS - 1)], sf_sem.at[0, 4])
    wait_for(recv_ft.at[0, pl.ds(0, 2 * COLS - 1)], sf_sem.at[0, 5])
    wait_for(recv_ft.at[1, pl.ds(0, COLS - 1)], sf_sem.at[0, 6])
    wait_for(recv_7.at[pl.ds(0, COLS - 1)], sb_sem.at[0, 7])
    wait_for(recv_6.at[pl.ds(0, 2 * COLS - 1)], sb_sem.at[0, 6])
    wait_for(recv_b5.at[pl.ds(0, 4 * COLS - 1)], sb_sem.at[0, 5])
    for t in range(1, SUB):
        for h in range(2):
            wait_for(recv_b.at[h, t, pl.ds(0, 2 * COLS - 1)], sb_sem.at[h, t])
    for h, value, copy in zip(streams, mine, last):
        copy.wait_send()
        copy.wait_recv()
        rows = pl.ds(pl.multiple_of(h * HALF, HALF), HALF)
        sub_out[0, rows] = value + last_in[h]


def hand_over(sub, top):
    def body(sub_in, top_in, sub_res, top_res, sems):
        copies = [
            pltpu.make_async_copy(sub_in, sub_res.at[0, 0, 0], sems.at[0]),
            pltpu.make_async_copy(top_in, top_res.at[0, 0], sems.at[1]),
        ]
        for copy in copies:
            copy.start()
        for copy in copies:
            copy.wait()

    any_spec = pl.BlockSpec(memory_space=pl.ANY)
    return pl.pallas_call(
        body,
        out_shape=(
            jax.ShapeDtypeStruct((1, 1, 1) + sub.shape, F32),
            jax.ShapeDtypeStruct((1, 1) + top.shape, F32),
        ),
        in_specs=[any_spec] * 2,
        out_specs=[any_spec] * 2,
        scratch_shapes=[pltpu.SemaphoreType.DMA((2,))],
    )(pltpu.with_memory_space_constraint(sub, pltpu.VMEM), pltpu.with_memory_space_constraint(top, pltpu.VMEM))


def local(*args):
    flat = [a.reshape(a.shape[3:] if i < 7 else a.shape[2:]) for i, a in enumerate(args)]
    flat[0] = args[0].reshape(SUB, 2, HALF, WIDTH)
    flat[5], flat[6] = (a.reshape(SUB, 1, SLOTS) for a in args[5:7])
    flat = [pltpu.with_memory_space_constraint(a, pltpu.HBM) for a in flat]
    vmem, smem, dma = pltpu.VMEM, pltpu.SMEM, pltpu.SemaphoreType.DMA
    tile = (SIDES, WIDTH)
    half = (HALF, WIDTH)
    block = (WIDTH, WIDTH)
    scratch = [
        smem((SUB, 1, SLOTS), jnp.int32),
        smem((SUB, 1, SLOTS), jnp.int32),
        smem((TOP - 1, SLOTS), jnp.int32),
        smem((TOP - 1, SLOTS), jnp.int32),
        vmem((SLOTS,) + block, BF16),
        vmem((LINKED, SLOTS) + block, BF16),
        vmem((LINKED, SLOTS) + block, BF16),
        vmem((SUB + TOP,) + block, F32),
        vmem((SUB + TOP,) + block, F32),
        vmem((SUB, 2) + half, F32),
        vmem((TOP,) + half, F32),
        vmem((6,) + block, BF16),
        vmem((LINKED,) + block, BF16),
        vmem((6,) + block, BF16),
        vmem((LINKED,) + block, BF16),
        vmem((2,) + block, BF16),
        vmem((SUB - 1, 2) + half, F32),
        vmem((2,) + half, F32),
        smem((LINKED, SLOTS), jnp.int32),
        smem((LINKED, SLOTS), jnp.int32),
        smem((LINKED, 2 * COLS + 1), jnp.int32),
        vmem((2, 2) + half, BF16),
        vmem((2, 2) + half, BF16),
        vmem((SUB, 2) + half, F32),
        vmem((TOP,) + half, F32),
        vmem((2, SLOTS + 1) + half, F32),
        vmem((2, COLS) + half, F32),
        vmem((COLS,) + half, F32),
        vmem((2, SUB - 1, COLS) + half, BF16),
        vmem((2, SUB - 1, 2 * COLS) + half, BF16),
        vmem((TOP, COLS) + half, BF16),
        vmem((4 * COLS,) + half, BF16),
        vmem((2, 2 * COLS) + half, BF16),
        vmem((2, COLS) + half, F32),
        vmem((2, COLS) + half, BF16),
        vmem((2, COLS) + half, BF16),
        vmem((2, COLS) + half, BF16),
        vmem((2, 7 * COLS) + half, BF16),
        vmem((2 * COLS,) + half, BF16),
        vmem((2, SUB, 2) + half, BF16),
        vmem((2, SUB, 2 * COLS) + half, BF16),
        vmem((TOP, 2) + half, BF16),
        vmem((COLS,) + half, BF16),
        vmem((2 * COLS,) + half, BF16),
        vmem((4 * COLS,) + half, BF16),
        vmem((COLS,) + half, BF16),
        vmem((COLS,) + half, BF16),
        vmem((2,) + half, F32),
        vmem((2,) + half, F32),
        vmem((TOP,) + half, F32),
        vmem((TOP,) + half, F32),
        vmem(block, BF16),
        dma((15,)),
        dma((6, LINKED)),
        pltpu.SemaphoreType.REGULAR((4,)),
        dma((10,)),
        dma((10,)),
        dma((2, SUB + TOP)),
        dma((2, SUB + TOP)),
        dma((2, SUB + TOP)),
        dma((2, SUB + TOP)),
    ]
    any_spec = pl.BlockSpec(memory_space=pl.ANY)
    vmem_spec = pl.BlockSpec(memory_space=pltpu.VMEM)
    sub, top = pl.pallas_call(
        kernel,
        out_shape=(
            jax.ShapeDtypeStruct((SUB,) + tile, F32),
            jax.ShapeDtypeStruct((TOP,) + tile, F32),
        ),
        in_specs=[any_spec] * 14,
        out_specs=(vmem_spec, vmem_spec),
        scratch_shapes=scratch,
        compiler_params=pltpu.CompilerParams(
            collective_id=0, has_side_effects=True, vmem_limit_bytes=48 * 1024 * 1024
        ),
    )(*flat)
    return hand_over(sub, top)


def solution(mesh):
    sub = P("layer", "prow", "pcol")
    top = P("prow", "pcol")
    return jax.shard_map(
        local, mesh=mesh, in_specs=(sub,) * 7 + (top,) * 7, out_specs=(sub, top), check_vma=False
    )
```
